256 devices in a mesh: rep: 8 (over x, core), dom: 32 (over y, z).
Axes of the slice: x: 4, y: 4, z: 8, core: 2. Of those that a mesh axis runs over, the one named last changes fastest.
Arguments:
- node_latent: bfloat16 [8, 16384, 256], P('rep', 'dom'), may hold values from -6 to 6
- edge_latent: bfloat16 [8, 131072, 256], P('rep', 'dom'), may hold values from -6 to 6
- node_cot: bfloat16 [8, 16384, 256], P('rep', 'dom'), may hold values from -6 to 6
- edge_cot: bfloat16 [8, 131072, 256], P('rep', 'dom'), may hold values from -6 to 6
- edge_w_in: bfloat16 [768, 256], replicated, may hold values from -0.21875 to 0.21875
- edge_b_in: float32 [256], replicated, may hold values from -3 to 3
- edge_w_out: bfloat16 [256, 256], replicated, may hold values from -0.375 to 0.375
- edge_gain: float32 [256], replicated, may hold values from 0.5 to 1.5
- node_w_in: bfloat16 [512, 256], replicated, may hold values from -0.25 to 0.25
- node_b_in: float32 [256], replicated, may hold values from -3 to 3
- node_w_out: bfloat16 [256, 256], replicated, may hold values from -0.375 to 0.375
- node_gain: float32 [256], replicated, may hold values from 0.5 to 1.5
- edge_senders: int32 [8, 131072], P('rep', 'dom'), may hold values from 0 to 767, as said below
- edge_receivers: int32 [8, 131072], P('rep', 'dom'), may hold values from 0 to 511, as said below
- block_fill: int32 [8, 1024], P('rep', 'dom'), may hold values from 0 to 128, as said below
- send_rows: int32 [8, 64, 128], P('rep', 'dom'), may hold values from 0 to 511, as said below
Outputs:
- grad_nodes: bfloat16 [8, 16384, 256], P('rep', 'dom')
- grad_edges: bfloat16 [8, 131072, 256], P('rep', 'dom')
- grad_edge_w_in: float32 [768, 256], P('dom')
- grad_edge_b_in: float32 [256], P('dom')
- grad_edge_w_out: float32 [256, 256], P('dom')
- grad_edge_gain: float32 [256], P('dom')
- grad_node_w_in: float32 [512, 256], P('dom')
- grad_node_b_in: float32 [256], P('dom')
- grad_node_w_out: float32 [256, 256], P('dom')
- grad_node_gain: float32 [256], P('dom')
The draws below stay inside these ranges and needn't reach their ends.
Inputs may be any that keep to these rules, and one draw needn't show every extreme that they name: Each partition has 32 blocks of 128 slots; blocks in use come first and every partition uses at least one; a block's first block_fill slots are live edges, the rest padding. `edge_receivers`: along a partition's live slots the receivers never fall; padding slots hold 0. `edge_senders`: rows of the partition's table: own rows, then the 128 rows from the lower neighbour, then the 128 from the upper; the first and last partitions never name a missing neighbour; padding slots hold 0. `send_rows`: for each partition, two lists of 128 distinct own rows: first those sent to the lower neighbour, then those sent to the upper.
All inputs are finite; a program needn't handle non-finite values.
Results may differ from the reference program's by a relative error of at most 0.01.
Values may be sent and summed in bfloat16 or wider, within the bound.
No kernel may reach another device: no remote copies, remote signals or barrier semaphores. Data moves between devices by JAX's collectives and lax.ppermute only.
A program may use at most 128 MiB of HBM per device.

```python
import jax
import jax.numpy as jnp
from jax import lax

D = 256
NODE_DEV = 512
EBLOCK = 128
GEOMS = 8
EDGE_DEV = 4096
HALO = 128
NBLK = 32
NODES = 16384
EDGES = 131072
SHARDS = 256
N_DOM = 32


def graph_tables(key):
    nblocks = EDGE_DEV // EBLOCK
    key_used, key_fill, key_full, key_gaps, key_slot, key_near, key_pick = jax.random.split(key, 7)
    used_blocks = jax.random.randint(key_used, (GEOMS, N_DOM), max(1, nblocks // 8), nblocks + 1)
    full_part = jax.random.randint(key_full, (GEOMS, 1), 0, N_DOM)
    is_full = jnp.arange(N_DOM)[None, :] == full_part
    used_blocks = jnp.where(is_full, nblocks, used_blocks)
    fills = jax.random.randint(key_fill, (GEOMS, N_DOM, nblocks), EBLOCK // 2, EBLOCK + 1)
    block_ids = jnp.arange(nblocks)[None, None, :]
    fills = jnp.where(is_full[:, :, None] & (block_ids == 0), EBLOCK, fills)
    fills = jnp.where(block_ids < used_blocks[:, :, None], fills, 0)
    slot_ids = jnp.arange(EBLOCK)[None, None, None, :]
    live_slots = (slot_ids < fills[..., None]).reshape(GEOMS, N_DOM, EDGE_DEV)
    live_int = live_slots.astype(jnp.int32)
    ranks = jnp.maximum(jnp.cumsum(live_int, -1) - 1, 0)
    live_total = jnp.sum(live_int, -1, keepdims=True)
    climbs = jnp.cumsum(jax.random.randint(key_gaps, (GEOMS, N_DOM, EDGE_DEV), 1, 4), -1)
    at_rank = jnp.take_along_axis(climbs, ranks, -1)
    ceiling = jnp.take_along_axis(climbs, live_total - 1, -1) + 1
    receivers = at_rank * NODE_DEV // ceiling
    shape_all = (GEOMS, N_DOM, EDGE_DEV)
    nearby = jnp.clip(receivers + jax.random.randint(key_near, shape_all, -8, 9), 0, NODE_DEV - 1)
    picked = jax.random.randint(key_pick, shape_all, 0, 4) == 0
    part_ids = jnp.arange(N_DOM)[None, :, None]
    low_side = receivers < NODE_DEV // 2
    halo_slots = jax.random.randint(key_slot, shape_all, 0, HALO)
    to_lower = picked & low_side & (part_ids > 0)
    to_upper = picked & jnp.logical_not(low_side) & (part_ids < N_DOM - 1)
    senders = jnp.where(to_lower, NODE_DEV + halo_slots, jnp.where(to_upper, NODE_DEV + HALO + halo_slots, nearby))
    senders = jnp.where(live_slots, senders, 0)
    receivers = jnp.where(live_slots, receivers, 0)
    return (fills.reshape(GEOMS, N_DOM * nblocks).astype(jnp.int32), senders.reshape(GEOMS, N_DOM * EDGE_DEV).astype(jnp.int32), receivers.reshape(GEOMS, N_DOM * EDGE_DEV).astype(jnp.int32))


def draw_block_fill(key, part):
    tables = graph_tables(key)
    return tables[0]


def draw_edge_senders(key, part):
    tables = graph_tables(key)
    return tables[1]


def draw_edge_receivers(key, part):
    tables = graph_tables(key)
    return tables[2]


def first_rows(row_key):
    return jax.random.permutation(row_key, 2 * HALO)[:HALO]


def draw_send_rows(key, part):
    key = jax.random.fold_in(key, 11)
    row_keys = jax.random.split(key, GEOMS * N_DOM * 2)
    picks = jax.vmap(first_rows)(row_keys).reshape(GEOMS, N_DOM, 2, HALO)
    sides = jnp.arange(2)[None, None, :, None]
    chosen = jnp.where(sides == 0, picks, NODE_DEV - 1 - picks)
    return chosen.reshape(GEOMS, N_DOM * 2, HALO).astype(jnp.int32)


def block_scale(own_key, shape, pieces, smallest, top_value):
    def one(position, blocks):
        draws = jax.random.uniform(jax.random.fold_in(jax.random.fold_in(own_key, 6), position), (blocks,), jnp.float32, smallest / len(pieces), top_value / len(pieces))
        return jnp.repeat(jnp.exp(draws), shape[position] // blocks).reshape((-1,) + (1,) * (len(shape) - position - 1))

    loudness = one(*pieces[0])
    for cut in pieces[1:]:
        loudness = loudness * one(*cut)
    return loudness


def bell_draw(key, shape, width, limit, pieces=(), kind=jnp.bfloat16):
    loudness = block_scale(key, shape, pieces, -0.22, 0.18) if pieces else 1.0
    array = jax.random.normal(key, shape, jnp.float32) * width * loudness
    return jnp.minimum(jnp.maximum(array, -limit), limit).astype(kind)


def setup_inputs(seed: int = 0) -> dict:
    splits = jax.random.split(jax.random.key(seed), 17)
    node_latent = bell_draw(splits[0], (GEOMS, NODES, D), 1.0, 6.0, ((0, 8), (1, 32)))
    edge_latent = bell_draw(splits[1], (GEOMS, EDGES, D), 1.0, 6.0, ((0, 8), (1, 32)))
    node_cot = bell_draw(splits[2], (GEOMS, NODES, D), 1.0, 6.0, ((0, 8), (1, 32)))
    edge_cot = bell_draw(splits[3], (GEOMS, EDGES, D), 1.0, 6.0, ((0, 8), (1, 32)))
    edge_w_in = bell_draw(splits[4], (3 * D, D), (3 * D) ** -0.5, 0.21875)
    edge_b_in = bell_draw(splits[5], (D,), 0.5, 3.0, (), jnp.float32)
    edge_w_out = bell_draw(splits[6], (D, D), D ** -0.5, 0.375)
    edge_gain = jnp.clip(1.0 + 0.1 * jax.random.normal(splits[7], (D,), jnp.float32), 0.5, 1.5)
    node_w_in = bell_draw(splits[8], (2 * D, D), (2 * D) ** -0.5, 0.25)
    node_b_in = bell_draw(splits[9], (D,), 0.5, 3.0, (), jnp.float32)
    node_w_out = bell_draw(splits[10], (D, D), D ** -0.5, 0.375)
    node_gain = jnp.clip(1.0 + 0.1 * jax.random.normal(splits[11], (D,), jnp.float32), 0.5, 1.5)
    edge_senders = draw_edge_senders(jax.random.fold_in(splits[16], 71), 0)
    edge_receivers = draw_edge_receivers(jax.random.fold_in(splits[16], 71), 0)
    block_fill = draw_block_fill(jax.random.fold_in(splits[16], 71), 0)
    send_rows = draw_send_rows(jax.random.fold_in(splits[16], 71), 0)
    return {"node_latent": node_latent, "edge_latent": edge_latent, "node_cot": node_cot, "edge_cot": edge_cot, "edge_w_in": edge_w_in, "edge_b_in": edge_b_in, "edge_w_out": edge_w_out, "edge_gain": edge_gain, "node_w_in": node_w_in, "node_b_in": node_b_in, "node_w_out": node_w_out, "node_gain": node_gain, "edge_senders": edge_senders, "edge_receivers": edge_receivers, "block_fill": block_fill, "send_rows": send_rows}


NORM_EPS = 1e-05

def norm_forward(values):
    centred = values - lax.optimization_barrier(jnp.mean(values, -1, keepdims=True))
    inverse = lax.rsqrt(lax.optimization_barrier(jnp.mean(centred * centred, -1, keepdims=True)) + NORM_EPS)
    return (centred * inverse, inverse)

def norm_backward(out_grad, normed, inverse, gain_vec):
    scaled = out_grad * gain_vec
    return inverse * (scaled - lax.optimization_barrier(jnp.mean(scaled, -1, keepdims=True)) - normed * lax.optimization_barrier(jnp.mean(scaled * normed, -1, keepdims=True)))

def silu_slope(values):
    sigma = jax.nn.sigmoid(values)
    return sigma * (1.0 + values * (1.0 - sigma))

def local_terms(node_rows, halo_rows, edge_rows, node_grad_in, edge_grad_in, senders, receivers, live_mask, weights):
    edge_w_in, edge_b_in, edge_w_out, edge_gain, node_w_in, node_b_in, node_w_out, node_gain = weights
    feat_width = node_rows.shape[1]
    node_total = node_rows.shape[0]
    table_rows = jnp.concatenate([node_rows, halo_rows], 0)
    edge_input = jnp.concatenate([edge_rows, table_rows[senders], node_rows[receivers]], 1)
    edge_pre = jnp.dot(edge_input, edge_w_in, preferred_element_type=jnp.float32) + edge_b_in
    edge_act = jax.nn.silu(edge_pre).astype(jnp.bfloat16)
    edge_out = jnp.dot(edge_act, edge_w_out, preferred_element_type=jnp.float32)
    edge_normed, edge_inv = norm_forward(edge_out)
    live_col = live_mask[:, None]
    message = live_col * (edge_rows.astype(jnp.float32) + edge_gain * edge_normed)
    aggregate = jax.ops.segment_sum(message, receivers, num_segments=node_total).astype(jnp.bfloat16)
    node_input = jnp.concatenate([node_rows, aggregate], 1)
    node_pre = jnp.dot(node_input, node_w_in, preferred_element_type=jnp.float32) + node_b_in
    node_act = jax.nn.silu(node_pre).astype(jnp.bfloat16)
    node_out = jnp.dot(node_act, node_w_out, preferred_element_type=jnp.float32)
    node_normed, node_inv = norm_forward(node_out)
    up_grad = node_grad_in.astype(jnp.float32)
    node_back = norm_backward(up_grad, node_normed, node_inv, node_gain).astype(jnp.bfloat16)
    node_act_grad = jnp.dot(node_back, node_w_out.T, preferred_element_type=jnp.float32)
    node_pre_grad = (node_act_grad * silu_slope(node_pre)).astype(jnp.bfloat16)
    node_input_grad = jnp.dot(node_pre_grad, node_w_in.T, preferred_element_type=jnp.float32)
    edge_msg_grad = live_col * (edge_grad_in.astype(jnp.float32) + node_input_grad[:, feat_width:][receivers])
    edge_back = norm_backward(edge_msg_grad, edge_normed, edge_inv, edge_gain).astype(jnp.bfloat16)
    edge_act_grad = jnp.dot(edge_back, edge_w_out.T, preferred_element_type=jnp.float32)
    edge_pre_grad = (edge_act_grad * silu_slope(edge_pre)).astype(jnp.bfloat16)
    edge_input_grad = jnp.dot(edge_pre_grad, edge_w_in.T, preferred_element_type=jnp.float32)
    edge_grad = (edge_msg_grad + edge_input_grad[:, :feat_width]).astype(jnp.bfloat16)
    table_grad = jax.ops.segment_sum(edge_input_grad[:, feat_width:2 * feat_width], senders, num_segments=table_rows.shape[0])
    recv_grad = jax.ops.segment_sum(edge_input_grad[:, 2 * feat_width:], receivers, num_segments=node_total)
    own_grad = up_grad + node_input_grad[:, :feat_width] + recv_grad + table_grad[:node_total]
    terms = (jnp.dot(edge_input.T, edge_pre_grad, preferred_element_type=jnp.float32), lax.optimization_barrier(jnp.sum(edge_pre_grad.astype(jnp.float32), 0)), jnp.dot(edge_act.T, edge_back, preferred_element_type=jnp.float32), lax.optimization_barrier(jnp.sum(edge_msg_grad * edge_normed, 0)), jnp.dot(node_input.T, node_pre_grad, preferred_element_type=jnp.float32), lax.optimization_barrier(jnp.sum(node_pre_grad.astype(jnp.float32), 0)), jnp.dot(node_act.T, node_back, preferred_element_type=jnp.float32), lax.optimization_barrier(jnp.sum(up_grad * node_normed, 0)))
    return (own_grad, table_grad[node_total:], edge_grad, terms)

def take_rows(row_table, row_picks):
    return row_table[row_picks]

def add_back(own_grad, send_lists, lower_part, upper_part):
    return own_grad.at[send_lists[0]].add(lower_part).at[send_lists[1]].add(upper_part)

def reference(node_latent, edge_latent, node_cot, edge_cot, edge_w_in, edge_b_in, edge_w_out, edge_gain, node_w_in, node_b_in, node_w_out, node_gain, edge_senders, edge_receivers, block_fill, send_rows):
    items = GEOMS * N_DOM
    node_blocks = node_latent.reshape(GEOMS, N_DOM, NODE_DEV, D)
    send_lists = send_rows.reshape(GEOMS, N_DOM, 2, HALO)
    outgoing = jax.vmap(jax.vmap(take_rows))(node_blocks, send_lists)
    zero_slab = jnp.zeros_like(outgoing[:, :1, 0])
    from_lower = jnp.concatenate([zero_slab, outgoing[:, :-1, 1]], 1)
    from_upper = jnp.concatenate([outgoing[:, 1:, 0], zero_slab], 1)
    halo_table = jnp.concatenate([from_lower, from_upper], 2).reshape(items, 2 * HALO, D)
    fills = block_fill.reshape(items, NBLK)
    live_mask = (jnp.arange(EBLOCK)[None, None, :] < fills[:, :, None]).reshape(items, EDGE_DEV).astype(jnp.float32)
    weights = (edge_w_in, edge_b_in, edge_w_out, edge_gain, node_w_in, node_b_in, node_w_out, node_gain)
    start = tuple((jnp.zeros(weight.shape, jnp.float32) for weight in weights))
    inputs = (node_latent.reshape(items, NODE_DEV, D), halo_table, edge_latent.reshape(items, EDGE_DEV, D), node_cot.reshape(items, NODE_DEV, D), edge_cot.reshape(items, EDGE_DEV, D), edge_senders.reshape(items, EDGE_DEV), edge_receivers.reshape(items, EDGE_DEV), live_mask)

    def one_part(totals, piece):
        own_grad, halo_grad, edge_grad, terms = local_terms(piece[0], piece[1], piece[2], piece[3], piece[4], piece[5], piece[6], piece[7], weights)
        totals = tuple((total + term for total, term in zip(totals, terms)))
        return (totals, (own_grad, halo_grad, edge_grad))
    totals, stacked = lax.scan(one_part, start, inputs)
    own_grads, halo_grads, edge_grads = stacked
    halo_parts = halo_grads.reshape(GEOMS, N_DOM, 2, HALO, D)
    zero_back = jnp.zeros_like(halo_parts[:, :1, 0])
    back_lower = jnp.concatenate([zero_back, halo_parts[:, :-1, 1]], 1)
    back_upper = jnp.concatenate([halo_parts[:, 1:, 0], zero_back], 1)
    own_grads = own_grads.reshape(GEOMS, N_DOM, NODE_DEV, D)
    own_grads = jax.vmap(jax.vmap(add_back))(own_grads, send_lists, back_lower, back_upper)
    grad_nodes = own_grads.reshape(GEOMS, NODES, D).astype(jnp.bfloat16)
    grad_edges = edge_grads.reshape(GEOMS, EDGES, D)
    means = tuple((total / SHARDS for total in totals))
    return (grad_nodes, grad_edges, means[0], means[1], means[2], means[3], means[4], means[5], means[6], means[7])
```

```python
import functools

import jax
import jax.numpy as jnp
from jax import lax
from jax.experimental import pallas as pl
from jax.experimental.pallas import tpu as pltpu
from jax.sharding import PartitionSpec as P

D = 256
NODE = 512
EDGE = 4096
HALO = 128
TABLE = NODE + 2 * HALO
EBLOCK = 128
NBLK = EDGE // EBLOCK
CHUNK = 512
NCHUNK = EDGE // CHUNK
PER = CHUNK // EBLOCK
SUB = 128
LANE = 128
NORM_EPS = 1e-05
N_DOM = 32
EDGE_ROWS = 40
NODE_ROWS = 32

BF = jnp.bfloat16
F32 = jnp.float32


def mm(a, b):
    return lax.dot_general(a, b, (((1,), (0,)), ((), ())), preferred_element_type=F32)


def mm_nt(a, b):
    return lax.dot_general(a, b, (((1,), (1,)), ((), ())), preferred_element_type=F32)


def mm_tn(a, b):
    return lax.dot_general(a, b, (((0,), (0,)), ((), ())), preferred_element_type=F32)


def as_columns(row):
    return jnp.broadcast_to(row, (LANE, LANE)).T


def one_hot_rows(row, count):
    places = lax.broadcasted_iota(jnp.int32, (count, row.shape[1]), 0)
    return jnp.where(places == row, 1.0, 0.0).astype(BF)


def one_hot_cols(cols, count):
    places = lax.broadcasted_iota(jnp.int32, (cols.shape[0], LANE), 1)
    parts = [
        jnp.where(cols == places + k * LANE, 1.0, 0.0).astype(BF) for k in range(count // LANE)
    ]
    return jnp.concatenate(parts, 1)


def norm_forward(values):
    centred = values - jnp.mean(values, -1, keepdims=True)
    inverse = lax.rsqrt(jnp.mean(centred * centred, -1, keepdims=True) + NORM_EPS)
    return centred * inverse, inverse


def pick_kernel(rows_ref, node_ref, low_ref, up_ref):
    for side, out in ((0, low_ref), (1, up_ref)):
        hot = one_hot_cols(as_columns(rows_ref[side : side + 1, :]), NODE)
        out[...] = mm(hot, node_ref[...]).astype(BF)


def layer_kernel(
    send_ref,
    recv_ref,
    fill_ref,
    edge_ref,
    ecot_ref,
    node_ref,
    hlow_ref,
    hup_ref,
    ncot_ref,
    ewi_ref,
    eb_ref,
    ewo_ref,
    eg_ref,
    nwi_ref,
    nb_ref,
    nwo_ref,
    ng_ref,
    gedge_ref,
    own_ref,
    glow_ref,
    gup_ref,
    edge_sum_ref,
    node_sum_ref,
    wp_ref,
    x_ref,
    hot_ref,
    hott_ref,
    act_ref,
    slope_ref,
    normed_ref,
    inv_ref,
    agg_ref,
    back_node_ref,
    sums_ref,
    sumr_ref,
    dw0_ref,
    dwo_ref,
    dgain_ref,
    base_ref,
):
    table = jnp.concatenate([node_ref[...], hlow_ref[...], hup_ref[...]], 0)
    wp_ref[0:D, :] = (ewi_ref[0:D, :].astype(F32) * 0.5).astype(BF)
    wp_ref[D : D + TABLE, :] = (mm(table, ewi_ref[D : 2 * D, :]) * 0.5).astype(BF)
    wp_ref[D + TABLE :, :] = (
        (mm(node_ref[...], ewi_ref[2 * D :, :]) + eb_ref[...]) * 0.5
    ).astype(BF)
    agg_ref[...] = jnp.zeros_like(agg_ref)
    gain = eg_ref[...]
    lanes = lax.broadcasted_iota(jnp.int32, (1, LANE), 1)

    def forward(i, carry):
        at = pl.multiple_of(i * CHUNK, CHUNK)
        parts = []
        for k in range(PER):
            here = pl.ds(pl.multiple_of(at + k * LANE, LANE), LANE)
            fill = fill_ref[0, i * PER + k]
            row = jnp.where(lanes < fill, recv_ref[:, here], -1)
            parts.append(row)
            cols = as_columns(row)
            hot = one_hot_cols(cols, NODE)
            rows = pl.ds(k * LANE, LANE)
            x_ref[rows, D + TABLE :] = hot
            hot_ref[here, :] = hot
            x_ref[rows, D : D + TABLE] = one_hot_cols(as_columns(send_ref[:, here]), TABLE)
            x_ref[rows, 0:D] = edge_ref[here, :]
        hott = one_hot_rows(jnp.concatenate(parts, 1), NODE)
        hott_ref[i] = hott
        half = mm(x_ref[...], wp_ref[...])
        t = jnp.tanh(half)
        ht = half * t
        act = (half + ht).astype(BF)
        slope = (t + 1.0) * ((half - ht) + 1.0)
        here = pl.ds(at, CHUNK)
        act_ref[here, :] = act
        slope_ref[here, :] = slope
        out = mm(act, ewo_ref[...])
        normed, inverse = norm_forward(out)
        normed_ref[here, :] = normed
        inv_ref[here, :] = jnp.broadcast_to(inverse, (CHUNK, LANE))
        message = (edge_ref[here, :].astype(F32) + gain * normed).astype(BF)
        agg_ref[...] += mm(hott, message)
        return carry

    lax.fori_loop(0, NCHUNK, forward, 0)

    agg = agg_ref[...].astype(BF)
    node = node_ref[...]
    half = (mm(node, nwi_ref[0:D, :]) + mm(agg, nwi_ref[D:, :]) + nb_ref[...]) * 0.5
    t = jnp.tanh(half)
    ht = half * t
    act = (half + ht).astype(BF)
    slope = (t + 1.0) * ((half - ht) + 1.0) * 0.5
    normed, inverse = norm_forward(mm(act, nwo_ref[...]))
    up = ncot_ref[...].astype(F32)
    c = up * ng_ref[...]
    back = (
        inverse
        * (
            c
            - jnp.mean(c, -1, keepdims=True)
            - normed * jnp.mean(c * normed, -1, keepdims=True)
        )
    ).astype(BF)
    pre_grad = (mm_nt(back, nwo_ref[...]) * slope).astype(BF)
    base_ref[...] = up + mm_nt(pre_grad, nwi_ref[0:D, :])
    back_node_ref[...] = mm_nt(pre_grad, nwi_ref[D:, :]).astype(BF)
    mean = 1.0 / 256.0

    def put(ref, row, block):
        size = block.shape[0] // N_DOM
        block = (block * mean).reshape(N_DOM, size, D)
        for side in range(2):
            ref[side, :, row : row + size, :] = block[:, :, side * LANE : (side + 1) * LANE]

    def put_vectors(ref, row, first, second):
        both = jnp.concatenate([first, second, jnp.zeros((6, D), F32)], 0) * mean
        for side in range(2):
            ref[side, :, row : row + 8, :] = jnp.broadcast_to(
                both[None, :, side * LANE : (side + 1) * LANE], (N_DOM, 8, LANE)
            )

    put(node_sum_ref, 0, jnp.concatenate([mm_tn(node, pre_grad), mm_tn(agg, pre_grad)], 0))
    put(node_sum_ref, 16, mm_tn(act, back))
    put_vectors(
        node_sum_ref,
        24,
        jnp.sum(pre_grad.astype(F32), 0, keepdims=True),
        jnp.sum(up * normed, 0, keepdims=True),
    )

    sums_ref[...] = jnp.zeros_like(sums_ref)
    sumr_ref[...] = jnp.zeros_like(sumr_ref)
    dw0_ref[...] = jnp.zeros_like(dw0_ref)
    dwo_ref[...] = jnp.zeros_like(dwo_ref)
    dgain_ref[...] = jnp.zeros_like(dgain_ref)
    wo_half = (ewo_ref[...].astype(F32) * 0.5).astype(BF)

    def backward(i, carry):
        at = pl.multiple_of(i * CHUNK, CHUNK)
        here = pl.ds(at, CHUNK)
        gathered = mm(hot_ref[here, :], back_node_ref[...])
        masks = []
        for k in range(PER):
            fill = fill_ref[0, i * PER + k]
            slots = lax.broadcasted_iota(jnp.int32, (LANE, D), 0)
            masks.append(slots < fill)
        live = jnp.concatenate(masks, 0)
        msg = jnp.where(live, ecot_ref[here, :].astype(F32), 0.0) + gathered
        normed = normed_ref[here, :]
        c = msg * gain
        q = c * normed
        dgain_ref[...] += jnp.sum(q.reshape(CHUNK // 8, 8, D), 0)
        inverse = inv_ref[here, :]
        inverse = jnp.concatenate([inverse, inverse], 1)
        back = (
            inverse
            * (c - jnp.mean(c, -1, keepdims=True) - normed * jnp.mean(q, -1, keepdims=True))
        ).astype(BF)
        pre_grad = (mm_nt(back, wo_half) * slope_ref[here, :]).astype(BF)
        gedge_ref[here, :] = (msg + mm_nt(pre_grad, ewi_ref[0:D, :])).astype(BF)
        dwo_ref[...] += mm_tn(act_ref[here, :], back)
        dw0_ref[...] += mm_tn(edge_ref[here, :], pre_grad)
        sums_ref[...] += mm(one_hot_rows(send_ref[:, here], TABLE), pre_grad)
        sumr_ref[...] += mm(hott_ref[i], pre_grad)
        return carry

    lax.fori_loop(0, NCHUNK, backward, 0)

    sums = sums_ref[...]
    sumr = sumr_ref[...].astype(BF)
    sums_bf = sums.astype(BF)
    put(
        edge_sum_ref,
        0,
        jnp.concatenate([dw0_ref[...], mm_tn(table, sums_bf), mm_tn(node, sumr)], 0),
    )
    put(edge_sum_ref, 24, dwo_ref[...])
    put_vectors(
        edge_sum_ref,
        32,
        jnp.sum(sums, 0, keepdims=True),
        jnp.sum(dgain_ref[...], 0, keepdims=True) / gain,
    )
    table_grad = mm_nt(sums_bf, ewi_ref[D : 2 * D, :])
    own_ref[...] = base_ref[...] + mm_nt(sumr, ewi_ref[2 * D :, :]) + table_grad[0:NODE]
    glow_ref[...] = table_grad[NODE : NODE + HALO].astype(BF)
    gup_ref[...] = table_grad[NODE + HALO :].astype(BF)


def finish_kernel(rows_ref, own_ref, low_ref, up_ref, out_ref):
    out_ref[...] = (
        own_ref[...]
        + mm(one_hot_rows(rows_ref[0:1, :], NODE), low_ref[...])
        + mm(one_hot_rows(rows_ref[1:2, :], NODE), up_ref[...])
    ).astype(BF)


def on_device(kernel, outs, scratch, in_smem, count):
    vmem = pl.BlockSpec(memory_space=pltpu.VMEM)
    smem = pl.BlockSpec(memory_space=pltpu.SMEM)
    return pl.pallas_call(
        kernel,
        out_shape=outs,
        in_specs=[smem if k in in_smem else vmem for k in range(count)],
        out_specs=jax.tree.map(lambda _: vmem, outs),
        scratch_shapes=scratch,
        compiler_params=pltpu.CompilerParams(vmem_limit_bytes=56 * 1024 * 1024),
    )


def shape(*dims, dtype=F32):
    return jax.ShapeDtypeStruct(dims, dtype)


def pick(rows, node):
    outs = (shape(HALO, D, dtype=BF),) * 2
    return on_device(pick_kernel, outs, [], (), 2)(rows, node)


def layer(*args):
    outs = (
        shape(EDGE, D, dtype=BF),
        shape(NODE, D),
        shape(HALO, D, dtype=BF),
        shape(HALO, D, dtype=BF),
        shape(2, N_DOM, EDGE_ROWS, LANE),
        shape(2, N_DOM, NODE_ROWS, LANE),
    )
    scratch = [
        pltpu.VMEM((D + TABLE + NODE, D), BF),
        pltpu.VMEM((CHUNK, D + TABLE + NODE), BF),
        pltpu.VMEM((EDGE, NODE), BF),
        pltpu.VMEM((NCHUNK, NODE, CHUNK), BF),
        pltpu.VMEM((EDGE, D), BF),
        pltpu.VMEM((EDGE, D), F32),
        pltpu.VMEM((EDGE, D), F32),
        pltpu.VMEM((EDGE, LANE), F32),
        pltpu.VMEM((NODE, D), F32),
        pltpu.VMEM((NODE, D), BF),
        pltpu.VMEM((TABLE, D), F32),
        pltpu.VMEM((NODE, D), F32),
        pltpu.VMEM((D, D), F32),
        pltpu.VMEM((D, D), F32),
        pltpu.VMEM((8, D), F32),
        pltpu.VMEM((NODE, D), F32),
    ]
    return on_device(layer_kernel, outs, scratch, (2,), 17)(*args)


def finish(rows, own, low, up):
    return on_device(finish_kernel, shape(NODE, D, dtype=BF), [], (), 4)(rows, own, low, up)


def swap(values, axis, flip):
    count = lax.axis_size(axis)
    return lax.ppermute(values, axis, [(i, i ^ flip) for i in range(count)])


def exchange_sum(values, axis, groups):
    parts = lax.all_to_all(values, axis, 0, 0, tiled=True, axis_index_groups=groups)
    return jnp.sum(parts.astype(F32), 0)


def reduce_shares(values):
    core = lax.axis_index("rep") % 2
    away = lax.dynamic_index_in_dim(values, 1 - core, 0, keepdims=False).astype(BF)
    kept = lax.dynamic_index_in_dim(values, core, 0, keepdims=False)
    values = kept + swap(away, "rep", 1).astype(F32)
    values = values.reshape((4, 8) + values.shape[1:]).astype(BF)
    same_z = [[y * 8 + z for y in range(4)] for z in range(8)]
    same_y = [[y * 8 + z for z in range(8)] for y in range(4)]
    values = exchange_sum(values, "dom", same_z)
    values = exchange_sum(values.astype(BF), "dom", same_y)
    others = [swap(values, "rep", flip) for flip in (2, 4, 6)]
    values = values + others[0] + others[1] + others[2]
    other = swap(values, "rep", 1)
    left = jnp.where(core == 0, values, other)
    right = jnp.where(core == 0, other, values)
    return jnp.concatenate([left, right], 1)


def per_device(
    node_latent,
    edge_latent,
    node_cot,
    edge_cot,
    edge_w_in,
    edge_b_in,
    edge_w_out,
    edge_gain,
    node_w_in,
    node_b_in,
    node_w_out,
    node_gain,
    edge_senders,
    edge_receivers,
    block_fill,
    send_rows,
):
    node_rows = node_latent[0]
    lists = send_rows[0]
    count = lax.axis_size("dom")
    rise = [(i, i + 1) for i in range(count - 1)]
    fall = [(i + 1, i) for i in range(count - 1)]
    to_lower, to_upper = pick(lists, node_rows)
    halo_lower = lax.ppermute(to_upper, "dom", rise)
    halo_upper = lax.ppermute(to_lower, "dom", fall)
    gedge, own, glow, gup, edge_sums, node_sums = layer(
        edge_senders,
        edge_receivers,
        block_fill,
        edge_latent[0],
        edge_cot[0],
        node_rows,
        halo_lower,
        halo_upper,
        node_cot[0],
        edge_w_in,
        edge_b_in[None],
        edge_w_out,
        edge_gain[None],
        node_w_in,
        node_b_in[None],
        node_w_out,
        node_gain[None],
    )
    back_upper = lax.ppermute(glow, "dom", fall)
    back_lower = lax.ppermute(gup, "dom", rise)
    grad_nodes = finish(lists, own, back_lower, back_upper)
    share = reduce_shares(jnp.concatenate([edge_sums, node_sums], 2))
    edge_share, node_share = share[:EDGE_ROWS], share[EDGE_ROWS:]
    spot = lax.axis_index("dom") * 8
    vectors = lax.dynamic_slice_in_dim(
        jnp.concatenate([edge_share[32:34], node_share[24:26]], 0), spot, 8, 1
    )
    return (
        grad_nodes[None],
        gedge[None],
        edge_share[0:24],
        vectors[0],
        edge_share[24:32],
        vectors[1],
        node_share[0:16],
        vectors[2],
        node_share[16:24],
        vectors[3],
    )


def solution(mesh):
    placed = (
        P("rep", "dom", None),
        P("rep", "dom", None),
        P("rep", "dom", None),
        P("rep", "dom", None),
        P(),
        P(),
        P(),
        P(),
        P(),
        P(),
        P(),
        P(),
        P("rep", "dom"),
        P("rep", "dom"),
        P("rep", "dom"),
        P("rep", "dom", None),
    )
    return jax.shard_map(
        per_device,
        mesh=mesh,
        in_specs=placed,
        out_specs=(
            P("rep", "dom", None),
            P("rep", "dom", None),
            P("dom", None),
            P("dom"),
            P("dom", None),
            P("dom"),
            P("dom", None),
            P("dom"),
            P("dom", None),
            P("dom"),
        ),
        check_vma=False,
    )
```

```python
import functools

import jax
import jax.numpy as jnp
from jax import lax
from jax.experimental import pallas as pl
from jax.experimental.pallas import tpu as pltpu
from jax.sharding import PartitionSpec as P

D = 256
NODE = 512
EDGE = 4096
HALO = 128
TABLE = NODE + 2 * HALO
EBLOCK = 128
NBLK = EDGE // EBLOCK
CHUNK = 1024
NCHUNK = EDGE // CHUNK
PER = CHUNK // EBLOCK
LANE = 128
NORM_EPS = 1e-05
N_DOM = 32
ROWS = 64
VECTOR_ROW = 56
WINDOW = 256

BF = jnp.bfloat16
F32 = jnp.float32


def mm(a, b):
    return lax.dot_general(a, b, (((1,), (0,)), ((), ())), preferred_element_type=F32)


def mm_nt(a, b):
    return lax.dot_general(a, b, (((1,), (1,)), ((), ())), preferred_element_type=F32)


def mm_tn(a, b):
    return lax.dot_general(a, b, (((0,), (0,)), ((), ())), preferred_element_type=F32)


def as_columns(row):
    return jnp.broadcast_to(row, (LANE, LANE)).T


def one_hot_rows(row, count):
    places = lax.broadcasted_iota(jnp.int32, (count, row.shape[1]), 0).astype(jnp.int16)
    row = jnp.broadcast_to(row, (16, row.shape[1])).astype(jnp.int16)[0:1]
    return jnp.where(places == row, BF(1.0), BF(0.0))


def one_hot_cols(cols, count):
    places = lax.broadcasted_iota(jnp.int32, (cols.shape[0], LANE), 1).astype(jnp.int16)
    cols = cols.astype(jnp.int16)
    parts = [
        jnp.where(cols == places + jnp.int16(k * LANE), BF(1.0), BF(0.0))
        for k in range(count // LANE)
    ]
    return jnp.concatenate(parts, 1)


def norm_forward(values):
    centred = values - jnp.mean(values, -1, keepdims=True)
    inverse = lax.rsqrt(jnp.mean(centred * centred, -1, keepdims=True) + NORM_EPS)
    return centred * inverse, inverse


def chunk_cols(row, first, count):
    row = row - first
    hots = [
        one_hot_cols(as_columns(row[:, k * LANE : (k + 1) * LANE]), count) for k in range(PER)
    ]
    return jnp.concatenate(hots, 0)


def live_lanes(fill_ref, i):
    lanes = lax.broadcasted_iota(jnp.int32, (1, LANE), 1)
    return jnp.concatenate([lanes < fill_ref[0, i * PER + k] for k in range(PER)], 1)


def chunk_used(fill_ref, i):
    total = fill_ref[0, i * PER]
    for k in range(1, PER):
        total = total + fill_ref[0, i * PER + k]
    return total > 0


def chunk_ids(send_ref, recv_ref, fill_ref, i):
    here = pl.ds(pl.multiple_of(i * CHUNK, CHUNK), CHUNK)
    live = live_lanes(fill_ref, i)
    send = send_ref[:, here]
    recv = recv_ref[:, here]
    own = send < NODE
    low = jnp.minimum(recv, jnp.where(own, send, NODE - 1))
    high = jnp.maximum(recv, jnp.where(own, send, 0))
    low = jnp.min(jnp.where(live, low, NODE - 1))
    high = jnp.max(jnp.where(live, high, 0))
    first = jnp.minimum((low // 16) * 16, NODE - WINDOW)
    fits = high < first + WINDOW
    first = pl.multiple_of(jnp.where(fits, first, 0), 16)
    return send, jnp.where(live, recv, -1), first, fits


def pick_kernel(rows_ref, node_ref, low_ref, up_ref):
    for side, out in ((0, low_ref), (1, up_ref)):
        hot = one_hot_cols(as_columns(rows_ref[side : side + 1, :]), NODE)
        out[...] = mm(hot, node_ref[...]).astype(BF)


def local_kernel(
    send_ref,
    recv_ref,
    fill_ref,
    edge_hbm,
    node_ref,
    ewi_ref,
    eb_ref,
    half_hbm,
    edge_ref,
    half_ref,
    wp_ref,
    in_sem,
    out_sem,
):
    def fetch(i):
        here = pl.ds(i * CHUNK, CHUNK)
        return pltpu.make_async_copy(edge_hbm.at[here], edge_ref.at[here], in_sem.at[i])

    def flush(i):
        here = pl.ds(i * CHUNK, CHUNK)
        return pltpu.make_async_copy(half_ref.at[here], half_hbm.at[here], out_sem.at[i])

    for i in range(NCHUNK):
        fetch(i).start()
    wp_ref[0:D, :] = (ewi_ref[0:D, :].astype(F32) * 0.5).astype(BF)
    wp_ref[D : D + NODE, :] = (mm(node_ref[...], ewi_ref[D : 2 * D, :]) * 0.5).astype(BF)
    wp_ref[D + NODE :, :] = (
        (mm(node_ref[...], ewi_ref[2 * D :, :]) + eb_ref[...]) * 0.5
    ).astype(BF)

    def step(i, carry):
        here = pl.ds(pl.multiple_of(i * CHUNK, CHUNK), CHUNK)
        fetch(i).wait()

        @pl.when(chunk_used(fill_ref, i))
        def _():
            send, recv, first, fits = chunk_ids(send_ref, recv_ref, fill_ref, i)

            def nodes_part(first):
                return mm(
                    chunk_cols(send, first, WINDOW), wp_ref[pl.ds(D + first, WINDOW), :]
                ) + mm(
                    chunk_cols(recv, first, WINDOW), wp_ref[pl.ds(D + NODE + first, WINDOW), :]
                )

            half_ref[here, :] = mm(edge_ref[here, :], wp_ref[0:D, :]) + nodes_part(first)

            @pl.when(jnp.logical_not(fits))
            def _():
                half_ref[here, :] += nodes_part(WINDOW)

        flush(i).start()
        return carry

    lax.fori_loop(0, NCHUNK, step, 0)
    for i in range(NCHUNK):
        flush(i).wait()


def layer_kernel(
    send_ref,
    recv_ref,
    fill_ref,
    core_ref,
    half_hbm,
    edge_hbm,
    ecot_hbm,
    node_ref,
    hlow_ref,
    hup_ref,
    ncot_ref,
    ewi_ref,
    ewo_ref,
    eg_ref,
    nwi_ref,
    nb_ref,
    nwo_ref,
    ng_ref,
    gedge_hbm,
    own_ref,
    glow_ref,
    gup_ref,
    away_ref,
    kept_ref,
    half_ref,
    edge_ref,
    ecot_ref,
    gedge_ref,
    halo_ref,
    hott_ref,
    act_ref,
    normed_ref,
    inv_ref,
    agg_ref,
    back_node_ref,
    msg_ref,
    grad_ref,
    sums_ref,
    sumr_ref,
    dw0_ref,
    dwo_ref,
    dgain_ref,
    base_ref,
    share_ref,
    half_sem,
    edge_sem,
    ecot_sem,
    out_sem,
):
    def copy_of(source, target, sems, i):
        here = pl.ds(i * CHUNK, CHUNK)
        return pltpu.make_async_copy(source.at[here], target.at[here], sems.at[i])

    copy_of(half_hbm, half_ref, half_sem, 0).start()
    copy_of(edge_hbm, edge_ref, edge_sem, 0).start()

    halo = jnp.concatenate([hlow_ref[...], hup_ref[...]], 0)
    halo_ref[...] = (mm(halo, ewi_ref[D : 2 * D, :]) * 0.5).astype(BF)
    agg_ref[...] = jnp.zeros_like(agg_ref)
    gain = eg_ref[...]

    def forward(i, carry):
        here = pl.ds(pl.multiple_of(i * CHUNK, CHUNK), CHUNK)
        copy_of(half_hbm, half_ref, half_sem, i).wait()
        copy_of(edge_hbm, edge_ref, edge_sem, i).wait()

        @pl.when(i + 1 < NCHUNK)
        def _():
            copy_of(half_hbm, half_ref, half_sem, i + 1).start()
            copy_of(edge_hbm, edge_ref, edge_sem, i + 1).start()

        copy_of(ecot_hbm, ecot_ref, ecot_sem, i).start()

        @pl.when(chunk_used(fill_ref, i))
        def _():
            send, recv, first, fits = chunk_ids(send_ref, recv_ref, fill_ref, i)
            half = half_ref[here, :] + mm(chunk_cols(send, NODE, 2 * HALO), halo_ref[...])
            t = jnp.tanh(half)
            ht = half * t
            act = (half + ht).astype(BF)
            act_ref[here, :] = act
            half_ref[here, :] = (t + 1.0) * ((half - ht) + 1.0)
            normed, inverse = norm_forward(mm(act, ewo_ref[...]))
            normed_ref[here, :] = normed
            inv_ref[here, :] = jnp.broadcast_to(inverse, (CHUNK, LANE))
            message = (edge_ref[here, :].astype(F32) + gain * normed).astype(BF)
            hott = one_hot_rows(recv - first, WINDOW)
            hott_ref[i] = hott
            agg_ref[pl.ds(first, WINDOW), :] += mm(hott, message)

            @pl.when(jnp.logical_not(fits))
            def _():
                again = (edge_ref[here, :].astype(F32) + gain * normed_ref[here, :]).astype(BF)
                agg_ref[WINDOW:, :] += mm(one_hot_rows(recv - WINDOW, WINDOW), again)

        return carry

    lax.fori_loop(0, NCHUNK, forward, 0)

    both = jnp.concatenate([node_ref[...], agg_ref[...].astype(BF)], 1)
    half = (mm(both, nwi_ref[...]) + nb_ref[...]) * 0.5
    t = jnp.tanh(half)
    ht = half * t
    act = (half + ht).astype(BF)
    slope = (t + 1.0) * ((half - ht) + 1.0) * 0.5
    normed, inverse = norm_forward(mm(act, nwo_ref[...]))
    up = ncot_ref[...].astype(F32)
    c = up * ng_ref[...]
    back = (
        inverse
        * (
            c
            - jnp.mean(c, -1, keepdims=True)
            - normed * jnp.mean(c * normed, -1, keepdims=True)
        )
    ).astype(BF)
    pre_grad = (mm_nt(back, nwo_ref[...]) * slope).astype(BF)
    input_grad = mm_nt(pre_grad, nwi_ref[...])
    base_ref[...] = up + input_grad[:, 0:D]
    back_node_ref[...] = input_grad[:, D:].astype(BF)
    mean = 1.0 / 256.0

    def put(row, block):
        size = block.shape[0] // N_DOM
        block = (block * mean).reshape(N_DOM, size, D)
        for side in range(2):
            share_ref[side, :, row : row + size, :] = block[:, :, side * LANE : (side + 1) * LANE]

    put(32, mm_tn(both, pre_grad))
    put(48, mm_tn(act, back))
    node_bias = jnp.sum(pre_grad.astype(F32), 0, keepdims=True)
    node_gain = jnp.sum(up * normed, 0, keepdims=True)

    sums_ref[...] = jnp.zeros_like(sums_ref)
    sumr_ref[...] = jnp.zeros_like(sumr_ref)
    dw0_ref[...] = jnp.zeros_like(dw0_ref)
    dwo_ref[...] = jnp.zeros_like(dwo_ref)
    dgain_ref[...] = jnp.zeros_like(dgain_ref)
    wo_half = (ewo_ref[...].astype(F32) * 0.5).astype(BF)

    def backward(i, carry):
        at = pl.multiple_of(i * CHUNK, CHUNK)
        here = pl.ds(at, CHUNK)
        copy_of(ecot_hbm, ecot_ref, ecot_sem, i).wait()
        used = chunk_used(fill_ref, i)

        @pl.when(used)
        def _():
            send, recv, first, fits = chunk_ids(send_ref, recv_ref, fill_ref, i)
            slots = lax.broadcasted_iota(jnp.int32, (LANE, D), 0)
            live = jnp.concatenate(
                [slots < fill_ref[0, i * PER + k] for k in range(PER)], 0
            )
            msg_ref[...] = jnp.where(live, ecot_ref[here, :].astype(F32), 0.0) + mm(
                chunk_cols(recv, first, WINDOW), back_node_ref[pl.ds(first, WINDOW), :]
            )

            @pl.when(jnp.logical_not(fits))
            def _():
                msg_ref[...] += mm(chunk_cols(recv, WINDOW, WINDOW), back_node_ref[WINDOW:, :])

            msg = msg_ref[...]
            normed = normed_ref[here, :]
            c = msg * gain
            q = c * normed
            dgain_ref[...] += jnp.sum(q.reshape(CHUNK // 8, 8, D), 0)
            inverse = inv_ref[here, :]
            inverse = jnp.concatenate([inverse, inverse], 1)
            back = (
                inverse
                * (c - jnp.mean(c, -1, keepdims=True) - normed * jnp.mean(q, -1, keepdims=True))
            ).astype(BF)
            pre_grad = (mm_nt(back, wo_half) * half_ref[here, :]).astype(BF)
            grad_ref[...] = pre_grad
            gedge_ref[here, :] = (msg + mm_nt(pre_grad, ewi_ref[0:D, :])).astype(BF)
            dwo_ref[...] += mm_tn(act_ref[here, :], back)
            dw0_ref[...] += mm_tn(edge_ref[here, :], pre_grad)
            hott = jnp.concatenate(
                [
                    hott_ref[i],
                    one_hot_rows(send - first, WINDOW),
                    one_hot_rows(send - NODE, 2 * HALO),
                ],
                0,
            )
            sums = mm(hott, pre_grad)
            sumr_ref[pl.ds(first, WINDOW), :] += sums[0:WINDOW]
            sums_ref[pl.ds(first, WINDOW), :] += sums[WINDOW : 2 * WINDOW]
            sums_ref[NODE:, :] += sums[2 * WINDOW :]

            @pl.when(jnp.logical_not(fits))
            def _():
                hott = jnp.concatenate(
                    [one_hot_rows(recv - WINDOW, WINDOW), one_hot_rows(send - WINDOW, WINDOW)], 0
                )
                sums = mm(hott, grad_ref[...])
                sumr_ref[WINDOW:, :] += sums[0:WINDOW]
                sums_ref[WINDOW : 2 * WINDOW, :] += sums[WINDOW:]

        @pl.when(jnp.logical_not(used))
        def _():
            gedge_ref[here, :] = jnp.zeros((CHUNK, D), BF)

        copy_of(gedge_ref, gedge_hbm, out_sem, i).start()
        return carry

    lax.fori_loop(0, NCHUNK, backward, 0)

    table = jnp.concatenate([node_ref[...], hlow_ref[...], hup_ref[...]], 0)
    sums = sums_ref[...]
    sumr = sumr_ref[...].astype(BF)
    sums_bf = sums.astype(BF)
    put(
        0,
        jnp.concatenate([dw0_ref[...], mm_tn(table, sums_bf), mm_tn(node_ref[...], sumr)], 0),
    )
    put(24, dwo_ref[...])
    vectors = (
        jnp.sum(sums, 0, keepdims=True),
        jnp.sum(dgain_ref[...], 0, keepdims=True) / gain,
        node_bias,
        node_gain,
    )
    place = lax.broadcasted_iota(jnp.int32, (N_DOM, D), 1) // 8
    mine = place == lax.broadcasted_iota(jnp.int32, (N_DOM, D), 0)
    spread = jnp.concatenate([jnp.where(mine, v * mean, 0.0) for v in vectors], 1)
    source = lax.broadcasted_iota(jnp.int32, (4 * D, LANE), 0)
    target = lax.broadcasted_iota(jnp.int32, (4 * D, LANE), 1)
    moves = jnp.where(target == (source // D) * 8 + source % 8, 1.0, 0.0).astype(BF)
    large = spread.astype(BF)
    row = mm(large, moves) + mm((spread - large.astype(F32)).astype(BF), moves)
    eight = lax.broadcasted_iota(jnp.int32, (N_DOM, 8, LANE), 1)
    share_ref[0, :, VECTOR_ROW:, :] = jnp.where(eight == 0, row[:, None, :], 0.0)
    share_ref[1, :, VECTOR_ROW:, :] = jnp.zeros((N_DOM, 8, LANE), F32)
    core = core_ref[0, 0]
    kept_ref[...] = share_ref[core]
    away_ref[...] = share_ref[1 - core].astype(BF)
    table_grad = mm_nt(sums_bf, ewi_ref[D : 2 * D, :])
    own_ref[...] = base_ref[...] + mm_nt(sumr, ewi_ref[2 * D :, :]) + table_grad[0:NODE]
    glow_ref[...] = table_grad[NODE : NODE + HALO].astype(BF)
    gup_ref[...] = table_grad[NODE + HALO :].astype(BF)
    for i in range(NCHUNK):
        copy_of(gedge_ref, gedge_hbm, out_sem, i).wait()


def finish_kernel(rows_ref, own_ref, low_ref, up_ref, out_ref):
    hots = jnp.concatenate(
        [one_hot_rows(rows_ref[0:1, :], NODE), one_hot_rows(rows_ref[1:2, :], NODE)], 1
    )
    parts = jnp.concatenate([low_ref[...], up_ref[...]], 0)
    out_ref[...] = (own_ref[...] + mm(hots, parts)).astype(BF)


def unpack_kernel(core_ref, mine_ref, other_ref, ewi_ref, ewo_ref, nwi_ref, nwo_ref, vec_ref):
    flip = core_ref[0, 0] == 1
    mine = mine_ref[...]
    other = other_ref[...]
    both = jnp.concatenate([jnp.where(flip, other, mine), jnp.where(flip, mine, other)], 1)
    ewi_ref[...] = both[0:24]
    ewo_ref[...] = both[24:32]
    nwi_ref[...] = both[32:48]
    nwo_ref[...] = both[48:56]
    vec_ref[...] = both[VECTOR_ROW : VECTOR_ROW + 8, 0:LANE]


def on_device(kernel, outs, scratch, specs, out_specs=None):
    vmem = pl.BlockSpec(memory_space=pltpu.VMEM)
    kinds = {
        "v": vmem,
        "s": pl.BlockSpec(memory_space=pltpu.SMEM),
        "a": pl.BlockSpec(memory_space=pl.ANY),
    }
    flat, tree = jax.tree.flatten(outs)
    out_specs = out_specs or "v" * len(flat)
    return pl.pallas_call(
        kernel,
        out_shape=outs,
        in_specs=[kinds[k] for k in specs],
        out_specs=jax.tree.unflatten(tree, [kinds[k] for k in out_specs]),
        scratch_shapes=scratch,
        compiler_params=pltpu.CompilerParams(vmem_limit_bytes=56 * 1024 * 1024),
    )


def shape(*dims, dtype=F32):
    return jax.ShapeDtypeStruct(dims, dtype)


def pick(rows, node):
    outs = (shape(HALO, D, dtype=BF),) * 2
    return on_device(pick_kernel, outs, [], "vv")(rows, node)


def local(*args):
    scratch = [
        pltpu.VMEM((EDGE, D), BF),
        pltpu.VMEM((EDGE, D), F32),
        pltpu.VMEM((D + 2 * NODE, D), BF),
        pltpu.SemaphoreType.DMA((NCHUNK,)),
        pltpu.SemaphoreType.DMA((NCHUNK,)),
    ]
    return on_device(local_kernel, shape(EDGE, D), scratch, "vvsavvv", "a")(*args)


def layer(*args):
    outs = (
        shape(EDGE, D, dtype=BF),
        shape(NODE, D),
        shape(HALO, D, dtype=BF),
        shape(HALO, D, dtype=BF),
        shape(N_DOM, ROWS, LANE, dtype=BF),
        shape(N_DOM, ROWS, LANE),
    )
    scratch = [
        pltpu.VMEM((EDGE, D), F32),
        pltpu.VMEM((EDGE, D), BF),
        pltpu.VMEM((EDGE, D), BF),
        pltpu.VMEM((EDGE, D), BF),
        pltpu.VMEM((2 * HALO, D), BF),
        pltpu.VMEM((NCHUNK, WINDOW, CHUNK), BF),
        pltpu.VMEM((EDGE, D), BF),
        pltpu.VMEM((EDGE, D), F32),
        pltpu.VMEM((EDGE, LANE), F32),
        pltpu.VMEM((NODE, D), F32),
        pltpu.VMEM((NODE, D), BF),
        pltpu.VMEM((CHUNK, D), F32),
        pltpu.VMEM((CHUNK, D), BF),
        pltpu.VMEM((TABLE, D), F32),
        pltpu.VMEM((NODE, D), F32),
        pltpu.VMEM((D, D), F32),
        pltpu.VMEM((D, D), F32),
        pltpu.VMEM((8, D), F32),
        pltpu.VMEM((NODE, D), F32),
        pltpu.VMEM((2, N_DOM, ROWS, LANE), F32),
        pltpu.SemaphoreType.DMA((NCHUNK,)),
        pltpu.SemaphoreType.DMA((NCHUNK,)),
        pltpu.SemaphoreType.DMA((NCHUNK,)),
        pltpu.SemaphoreType.DMA((NCHUNK,)),
    ]
    return on_device(layer_kernel, outs, scratch, "vvssaaavvvvvvvvvvv", "avvvvv")(*args)


def finish(rows, own, low, up):
    return on_device(finish_kernel, shape(NODE, D, dtype=BF), [], "vvvv")(rows, own, low, up)


def unpack(core, mine, other):
    outs = (shape(24, D), shape(8, D), shape(16, D), shape(8, D), shape(8, LANE))
    return on_device(unpack_kernel, outs, [], "svv")(core, mine, other)


def swap(values, axis, flip):
    count = lax.axis_size(axis)
    return lax.ppermute(values, axis, [(i, i ^ flip) for i in range(count)])


def exchange_sum(values, axis, groups):
    parts = lax.all_to_all(values, axis, 0, 0, tiled=True, axis_index_groups=groups)
    return jnp.sum(parts.astype(F32), 0)


def per_device(
    node_latent,
    edge_latent,
    node_cot,
    edge_cot,
    edge_w_in,
    edge_b_in,
    edge_w_out,
    edge_gain,
    node_w_in,
    node_b_in,
    node_w_out,
    node_gain,
    edge_senders,
    edge_receivers,
    block_fill,
    send_rows,
):
    node_rows = node_latent[0]
    lists = send_rows[0]
    count = lax.axis_size("dom")
    rise = [(i, i + 1) for i in range(count - 1)]
    fall = [(i + 1, i) for i in range(count - 1)]
    core = lax.rem(lax.axis_index("rep"), 2).reshape(1, 1)
    to_lower, to_upper = pick(lists, node_rows)
    halo_lower = lax.ppermute(to_upper, "dom", rise)
    halo_upper = lax.ppermute(to_lower, "dom", fall)
    half = local(
        edge_senders,
        edge_receivers,
        block_fill,
        edge_latent[0],
        node_rows,
        edge_w_in,
        edge_b_in[None],
    )
    gedge, own, glow, gup, away, kept = layer(
        edge_senders,
        edge_receivers,
        block_fill,
        core,
        half,
        edge_latent[0],
        edge_cot[0],
        node_rows,
        halo_lower,
        halo_upper,
        node_cot[0],
        edge_w_in,
        edge_w_out,
        edge_gain[None],
        node_w_in,
        node_b_in[None],
        node_w_out,
        node_gain[None],
    )
    back_upper = lax.ppermute(glow, "dom", fall)
    back_lower = lax.ppermute(gup, "dom", rise)
    same_z = [[y * 8 + z for y in range(4)] for z in range(8)]
    same_y = [[y * 8 + z for z in range(8)] for y in range(4)]
    values = (kept + swap(away, "rep", 1).astype(F32)).astype(BF)
    values = exchange_sum(values.reshape(4, 8, ROWS, LANE), "dom", same_z).astype(BF)
    values, back_lower, back_upper = lax.optimization_barrier((values, back_lower, back_upper))
    values = exchange_sum(values, "dom", same_y)
    others = [swap(values, "rep", flip) for flip in (2, 4, 6)]
    grad_nodes = finish(lists, own, back_lower, back_upper)
    values = values + others[0] + others[1] + others[2]
    ewi, ewo, nwi, nwo, vec = unpack(core, values, swap(values, "rep", 1))
    return (
        grad_nodes[None],
        gedge[None],
        ewi,
        vec[0, 0:8],
        ewo,
        vec[0, 8:16],
        nwi,
        vec[0, 16:24],
        nwo,
        vec[0, 24:32],
    )


def solution(mesh):
    placed = (
        P("rep", "dom", None),
        P("rep", "dom", None),
        P("rep", "dom", None),
        P("rep", "dom", None),
        P(),
        P(),
        P(),
        P(),
        P(),
        P(),
        P(),
        P(),
        P("rep", "dom"),
        P("rep", "dom"),
        P("rep", "dom"),
        P("rep", "dom", None),
    )
    return jax.shard_map(
        per_device,
        mesh=mesh,
        in_specs=placed,
        out_specs=(
            P("rep", "dom", None),
            P("rep", "dom", None),
            P("dom", None),
            P("dom"),
            P("dom", None),
            P("dom"),
            P("dom", None),
            P("dom"),
            P("dom", None),
            P("dom"),
        ),
        check_vma=False,
    )
```

```python
import functools

import jax
import jax.numpy as jnp
from jax import lax
from jax.experimental import pallas as pl
from jax.experimental.pallas import tpu as pltpu
from jax.sharding import PartitionSpec as P

D = 256
NODE = 512
EDGE = 4096
HALO = 128
TABLE = NODE + 2 * HALO
EBLOCK = 128
NBLK = EDGE // EBLOCK
CHUNK = 1024
NCHUNK = EDGE // CHUNK
PER = CHUNK // EBLOCK
LANE = 128
NORM_EPS = 1e-05
N_DOM = 32
ROWS = 64
VECTOR_ROW = 56
WINDOW = 256

BF = jnp.bfloat16
F32 = jnp.float32


def mm(a, b):
    return lax.dot_general(a, b, (((1,), (0,)), ((), ())), preferred_element_type=F32)


def mm_nt(a, b):
    return lax.dot_general(a, b, (((1,), (1,)), ((), ())), preferred_element_type=F32)


def mm_tn(a, b):
    return lax.dot_general(a, b, (((0,), (0,)), ((), ())), preferred_element_type=F32)


def as_columns(row):
    return jnp.broadcast_to(row, (LANE, LANE)).T


def one_hot_rows(row, count):
    places = lax.broadcasted_iota(jnp.int32, (count, row.shape[1]), 0).astype(jnp.int16)
    row = jnp.broadcast_to(row, (16, row.shape[1])).astype(jnp.int16)[0:1]
    return jnp.where(places == row, BF(1.0), BF(0.0))


def one_hot_cols(cols, count):
    places = lax.broadcasted_iota(jnp.int32, (cols.shape[0], LANE), 1).astype(jnp.int16)
    cols = cols.astype(jnp.int16)
    parts = [
        jnp.where(cols == places + jnp.int16(k * LANE), BF(1.0), BF(0.0))
        for k in range(count // LANE)
    ]
    return jnp.concatenate(parts, 1)


def norm_forward(values):
    centred = values - jnp.mean(values, -1, keepdims=True)
    inverse = lax.rsqrt(jnp.mean(centred * centred, -1, keepdims=True) + NORM_EPS)
    return centred * inverse, inverse


def chunk_cols(row, first, count):
    row = row - first
    hots = [
        one_hot_cols(as_columns(row[:, k * LANE : (k + 1) * LANE]), count) for k in range(PER)
    ]
    return jnp.concatenate(hots, 0)


def live_lanes(fill_ref, i):
    lanes = lax.broadcasted_iota(jnp.int32, (1, LANE), 1)
    return jnp.concatenate([lanes < fill_ref[0, i * PER + k] for k in range(PER)], 1)


def chunk_used(fill_ref, i):
    total = fill_ref[0, i * PER]
    for k in range(1, PER):
        total = total + fill_ref[0, i * PER + k]
    return total > 0


def chunk_ids(send_ref, recv_ref, fill_ref, i):
    here = pl.ds(i * CHUNK, CHUNK)
    return send_ref[:, here], jnp.where(live_lanes(fill_ref, i), recv_ref[:, here], -1)


def windows(send_ref, recv_ref, fill_ref):
    firsts, all_fit = [], None
    for i in range(NCHUNK):
        here = pl.ds(i * CHUNK, CHUNK)
        live = live_lanes(fill_ref, i)
        send = send_ref[:, here]
        recv = recv_ref[:, here]
        own = send < NODE
        low = jnp.minimum(recv, jnp.where(own, send, NODE - 1))
        high = jnp.maximum(recv, jnp.where(own, send, 0))
        low = jnp.min(jnp.where(live, low, NODE - 1))
        high = jnp.max(jnp.where(live, high, 0))
        first = jnp.minimum((low // 16) * 16, NODE - WINDOW)
        fits = high < first + WINDOW
        firsts.append(pl.multiple_of(first, 16))
        all_fit = fits if all_fit is None else jnp.logical_and(all_fit, fits)
    return firsts, all_fit


def over_chunks(step, idle, fill_ref, firsts):
    if firsts is not None:
        for i in range(NCHUNK):
            step(i, firsts[i], WINDOW)
        return
    for i in range(NCHUNK - 1):
        step(i, 0, NODE)
    used = chunk_used(fill_ref, NCHUNK - 1)

    @pl.when(used)
    def _():
        step(NCHUNK - 1, 0, NODE)

    @pl.when(jnp.logical_not(used))
    def _():
        idle(NCHUNK - 1)


def either_way(body, send_ref, recv_ref, fill_ref):
    firsts, all_fit = windows(send_ref, recv_ref, fill_ref)

    @pl.when(all_fit)
    def _():
        body(firsts)

    @pl.when(jnp.logical_not(all_fit))
    def _():
        body(None)


def fetch_all(sources, targets, sems):
    copies = [
        pltpu.make_async_copy(source, target, sems.at[k])
        for k, (source, target) in enumerate(zip(sources, targets))
    ]
    for copy in copies:
        copy.start()
    return copies


def pick_kernel(rows_hbm, node_hbm, low_ref, up_ref, rows_ref, node_ref, sems):
    for copy in fetch_all((rows_hbm, node_hbm), (rows_ref, node_ref), sems):
        copy.wait()
    for side, out in ((0, low_ref), (1, up_ref)):
        hot = one_hot_cols(as_columns(rows_ref[side : side + 1, :]), NODE)
        out[...] = mm(hot, node_ref[...]).astype(BF)


def local_kernel(
    send_hbm,
    recv_hbm,
    fill_hbm,
    edge_hbm,
    node_hbm,
    ewi_hbm,
    eb_hbm,
    half_ref,
    send_ref,
    recv_ref,
    fill_ref,
    edge_ref,
    node_ref,
    ewi_ref,
    eb_ref,
    wp_ref,
    sems,
):
    copies = fetch_all(
        (node_hbm, ewi_hbm, eb_hbm, send_hbm, recv_hbm, fill_hbm, edge_hbm),
        (node_ref, ewi_ref, eb_ref, send_ref, recv_ref, fill_ref, edge_ref),
        sems,
    )
    for copy in copies[:-1]:
        copy.wait()
    wp_ref[0:D, :] = (ewi_ref[0:D, :].astype(F32) * 0.5).astype(BF)
    wp_ref[D : D + NODE, :] = (mm(node_ref[...], ewi_ref[D : 2 * D, :]) * 0.5).astype(BF)
    wp_ref[D + NODE :, :] = (
        (mm(node_ref[...], ewi_ref[2 * D :, :]) + eb_ref[...]) * 0.5
    ).astype(BF)

    def step(i, first, width):
        here = pl.ds(i * CHUNK, CHUNK)
        send, recv = chunk_ids(send_ref, recv_ref, fill_ref, i)
        half_ref[here, :] = (
            mm(edge_ref[here, :], wp_ref[0:D, :])
            + mm(chunk_cols(send, first, width), wp_ref[pl.ds(D + first, width), :])
            + mm(chunk_cols(recv, first, width), wp_ref[pl.ds(D + NODE + first, width), :])
        )

    def body(firsts):
        over_chunks(step, lambda i: None, fill_ref, firsts)

    copies[-1].wait()
    either_way(body, send_ref, recv_ref, fill_ref)


def layer_kernel(
    send_ref,
    recv_ref,
    fill_ref,
    core_ref,
    half_ref,
    edge_ref,
    ecot_ref,
    node_ref,
    hlow_ref,
    hup_ref,
    ncot_ref,
    ewi_ref,
    ewo_ref,
    eg_ref,
    nwi_ref,
    nb_ref,
    nwo_ref,
    ng_ref,
    gedge_hbm,
    own_ref,
    glow_ref,
    gup_ref,
    away_ref,
    kept_ref,
    slope_ref,
    gedge_ref,
    halo_ref,
    hott_ref,
    act_ref,
    normed_ref,
    inv_ref,
    agg_ref,
    back_node_ref,
    sums_ref,
    sumr_ref,
    dw0_ref,
    dwo_ref,
    dgain_ref,
    base_ref,
    share_ref,
    out_sem,
):
    def body(firsts):
        def copy_of(source, target, sems, i):
            here = pl.ds(i * CHUNK, CHUNK)
            return pltpu.make_async_copy(source.at[here], target.at[here], sems.at[i])


        halo = jnp.concatenate([hlow_ref[...], hup_ref[...]], 0)
        halo_ref[...] = (mm(halo, ewi_ref[D : 2 * D, :]) * 0.5).astype(BF)
        agg_ref[...] = jnp.zeros_like(agg_ref)
        gain = eg_ref[...]

        def forward(i, first, width):
            here = pl.ds(i * CHUNK, CHUNK)
            send, recv = chunk_ids(send_ref, recv_ref, fill_ref, i)
            half = half_ref[here, :] + mm(chunk_cols(send, NODE, 2 * HALO), halo_ref[...])
            t = jnp.tanh(half)
            ht = half * t
            act = (half + ht).astype(BF)
            act_ref[here, :] = act
            slope_ref[here, :] = (t + 1.0) * ((half - ht) + 1.0)
            normed, inverse = norm_forward(mm(act, ewo_ref[...]))
            normed_ref[here, :] = normed
            inv_ref[here, :] = jnp.broadcast_to(inverse, (CHUNK, LANE))
            message = (edge_ref[here, :].astype(F32) + gain * normed).astype(BF)
            hott = one_hot_rows(recv - first, width)
            hott_ref[i, 0:width, :] = hott
            agg_ref[pl.ds(first, width), :] += mm(hott, message)

        over_chunks(forward, lambda i: None, fill_ref, firsts)

        both = jnp.concatenate([node_ref[...], agg_ref[...].astype(BF)], 1)
        half = (mm(both, nwi_ref[...]) + nb_ref[...]) * 0.5
        t = jnp.tanh(half)
        ht = half * t
        act = (half + ht).astype(BF)
        slope = (t + 1.0) * ((half - ht) + 1.0) * 0.5
        normed, inverse = norm_forward(mm(act, nwo_ref[...]))
        up = ncot_ref[...].astype(F32)
        c = up * ng_ref[...]
        back = (
            inverse
            * (
                c
                - jnp.mean(c, -1, keepdims=True)
                - normed * jnp.mean(c * normed, -1, keepdims=True)
            )
        ).astype(BF)
        pre_grad = (mm_nt(back, nwo_ref[...]) * slope).astype(BF)
        input_grad = mm_nt(pre_grad, nwi_ref[...])
        base_ref[...] = up + input_grad[:, 0:D]
        back_node_ref[...] = input_grad[:, D:].astype(BF)
        mean = 1.0 / 256.0

        def put(row, block):
            size = block.shape[0] // N_DOM
            block = (block * mean).reshape(N_DOM, size, D)
            for side in range(2):
                share_ref[side, :, row : row + size, :] = block[:, :, side * LANE : (side + 1) * LANE]

        put(32, mm_tn(both, pre_grad))
        put(48, mm_tn(act, back))
        node_bias = jnp.sum(pre_grad.astype(F32), 0, keepdims=True)
        node_gain = jnp.sum(up * normed, 0, keepdims=True)

        sums_ref[...] = jnp.zeros_like(sums_ref)
        sumr_ref[...] = jnp.zeros_like(sumr_ref)
        dw0_ref[...] = jnp.zeros_like(dw0_ref)
        dwo_ref[...] = jnp.zeros_like(dwo_ref)
        dgain_ref[...] = jnp.zeros_like(dgain_ref)
        wo_half = (ewo_ref[...].astype(F32) * 0.5).astype(BF)

        def backward(i, first, width):
            here = pl.ds(i * CHUNK, CHUNK)
            send, recv = chunk_ids(send_ref, recv_ref, fill_ref, i)
            slots = lax.broadcasted_iota(jnp.int32, (LANE, D), 0)
            live = jnp.concatenate([slots < fill_ref[0, i * PER + k] for k in range(PER)], 0)
            msg = jnp.where(live, ecot_ref[here, :].astype(F32), 0.0) + mm(
                chunk_cols(recv, first, width), back_node_ref[pl.ds(first, width), :]
            )
            normed = normed_ref[here, :]
            c = msg * gain
            q = c * normed
            dgain_ref[...] += jnp.sum(q.reshape(CHUNK // 8, 8, D), 0)
            inverse = inv_ref[here, :]
            inverse = jnp.concatenate([inverse, inverse], 1)
            back = (
                inverse
                * (c - jnp.mean(c, -1, keepdims=True) - normed * jnp.mean(q, -1, keepdims=True))
            ).astype(BF)
            pre_grad = (mm_nt(back, wo_half) * slope_ref[here, :]).astype(BF)
            gedge_ref[here, :] = (msg + mm_nt(pre_grad, ewi_ref[0:D, :])).astype(BF)
            dwo_ref[...] += mm_tn(act_ref[here, :], back)
            dw0_ref[...] += mm_tn(edge_ref[here, :], pre_grad)
            hott = jnp.concatenate(
                [
                    hott_ref[i, 0:width, :],
                    one_hot_rows(send - first, width),
                    one_hot_rows(send - NODE, 2 * HALO),
                ],
                0,
            )
            sums = mm(hott, pre_grad)
            sumr_ref[pl.ds(first, width), :] += sums[0:width]
            sums_ref[pl.ds(first, width), :] += sums[width : 2 * width]
            sums_ref[NODE:, :] += sums[2 * width :]

        def padding(i):
            gedge_ref[pl.ds(i * CHUNK, CHUNK), :] = jnp.zeros((CHUNK, D), BF)

        over_chunks(backward, padding, fill_ref, firsts)
        for i in range(NCHUNK):
            copy_of(gedge_ref, gedge_hbm, out_sem, i).start()

        table = jnp.concatenate([node_ref[...], hlow_ref[...], hup_ref[...]], 0)
        sums = sums_ref[...]
        sumr = sumr_ref[...].astype(BF)
        sums_bf = sums.astype(BF)
        put(
            0,
            jnp.concatenate([dw0_ref[...], mm_tn(table, sums_bf), mm_tn(node_ref[...], sumr)], 0),
        )
        put(24, dwo_ref[...])
        vectors = (
            jnp.sum(sums, 0, keepdims=True),
            jnp.sum(dgain_ref[...], 0, keepdims=True) / gain,
            node_bias,
            node_gain,
        )
        place = lax.broadcasted_iota(jnp.int32, (N_DOM, D), 1) // 8
        mine = place == lax.broadcasted_iota(jnp.int32, (N_DOM, D), 0)
        spread = jnp.concatenate([jnp.where(mine, v * mean, 0.0) for v in vectors], 1)
        source = lax.broadcasted_iota(jnp.int32, (4 * D, LANE), 0)
        target = lax.broadcasted_iota(jnp.int32, (4 * D, LANE), 1)
        moves = jnp.where(target == (source // D) * 8 + source % 8, 1.0, 0.0).astype(BF)
        large = spread.astype(BF)
        row = mm(large, moves) + mm((spread - large.astype(F32)).astype(BF), moves)
        eight = lax.broadcasted_iota(jnp.int32, (N_DOM, 8, LANE), 1)
        share_ref[0, :, VECTOR_ROW:, :] = jnp.where(eight == 0, row[:, None, :], 0.0)
        share_ref[1, :, VECTOR_ROW:, :] = jnp.zeros((N_DOM, 8, LANE), F32)
        core = core_ref[0, 0]
        kept_ref[...] = share_ref[core]
        away_ref[...] = share_ref[1 - core].astype(BF)
        table_grad = mm_nt(sums_bf, ewi_ref[D : 2 * D, :])
        own_ref[...] = base_ref[...] + mm_nt(sumr, ewi_ref[2 * D :, :]) + table_grad[0:NODE]
        glow_ref[...] = table_grad[NODE : NODE + HALO].astype(BF)
        gup_ref[...] = table_grad[NODE + HALO :].astype(BF)
        for i in range(NCHUNK):
            copy_of(gedge_ref, gedge_hbm, out_sem, i).wait()

    either_way(body, send_ref, recv_ref, fill_ref)


def finish_kernel(rows_ref, own_ref, low_ref, up_ref, out_ref):
    hots = jnp.concatenate(
        [one_hot_rows(rows_ref[0:1, :], NODE), one_hot_rows(rows_ref[1:2, :], NODE)], 1
    )
    parts = jnp.concatenate([low_ref[...], up_ref[...]], 0)
    out_ref[...] = (own_ref[...] + mm(hots, parts)).astype(BF)


def unpack_kernel(core_ref, mine_ref, other_ref, ewi_ref, ewo_ref, nwi_ref, nwo_ref, *vec_refs):
    flip = core_ref[0, 0] == 1
    mine = mine_ref[...]
    other = other_ref[...]
    both = jnp.concatenate([jnp.where(flip, other, mine), jnp.where(flip, mine, other)], 1)
    ewi_ref[...] = both[0:24]
    ewo_ref[...] = both[24:32]
    nwi_ref[...] = both[32:48]
    nwo_ref[...] = both[48:56]
    for k in range(4):
        vec_refs[k][...] = both[VECTOR_ROW : VECTOR_ROW + 1, 8 * k : 8 * k + 8]


def on_device(kernel, outs, scratch, specs, out_specs=None, megabytes=8):
    vmem = pl.BlockSpec(memory_space=pltpu.VMEM)
    kinds = {
        "v": vmem,
        "s": pl.BlockSpec(memory_space=pltpu.SMEM),
        "a": pl.BlockSpec(memory_space=pl.ANY),
        "h": pl.BlockSpec(memory_space=pltpu.HBM),
    }
    flat, tree = jax.tree.flatten(outs)
    out_specs = out_specs or "v" * len(flat)
    return pl.pallas_call(
        kernel,
        out_shape=outs,
        in_specs=[kinds[k] for k in specs],
        out_specs=jax.tree.unflatten(tree, [kinds[k] for k in out_specs]),
        scratch_shapes=scratch,
        compiler_params=pltpu.CompilerParams(vmem_limit_bytes=megabytes * 1024 * 1024),
    )


def in_hbm(*args):
    return [pltpu.with_memory_space_constraint(a, pltpu.HBM) for a in args]


def shape(*dims, dtype=F32):
    return jax.ShapeDtypeStruct(dims, dtype)


def pick(rows, node):
    outs = (shape(HALO, D, dtype=BF),) * 2
    scratch = [
        pltpu.VMEM((2, HALO), jnp.int32),
        pltpu.VMEM((NODE, D), BF),
        pltpu.SemaphoreType.DMA((2,)),
    ]
    return on_device(pick_kernel, outs, scratch, "hh")(*in_hbm(rows, node))


def local(*args):
    scratch = [
        pltpu.VMEM((1, EDGE), jnp.int32),
        pltpu.VMEM((1, EDGE), jnp.int32),
        pltpu.SMEM((1, NBLK), jnp.int32),
        pltpu.VMEM((EDGE, D), BF),
        pltpu.VMEM((NODE, D), BF),
        pltpu.VMEM((3 * D, D), BF),
        pltpu.VMEM((1, D), F32),
        pltpu.VMEM((D + 2 * NODE, D), BF),
        pltpu.SemaphoreType.DMA((7,)),
    ]
    return on_device(local_kernel, shape(EDGE, D), scratch, "hhhhhhh", "v", 16)(*in_hbm(*args))


def layer(*args):
    outs = (
        shape(EDGE, D, dtype=BF),
        shape(NODE, D),
        shape(HALO, D, dtype=BF),
        shape(HALO, D, dtype=BF),
        shape(N_DOM, ROWS, LANE, dtype=BF),
        shape(N_DOM, ROWS, LANE),
    )
    scratch = [
        pltpu.VMEM((EDGE, D), F32),
        pltpu.VMEM((EDGE, D), BF),
        pltpu.VMEM((2 * HALO, D), BF),
        pltpu.VMEM((NCHUNK, NODE, CHUNK), BF),
        pltpu.VMEM((EDGE, D), BF),
        pltpu.VMEM((EDGE, D), F32),
        pltpu.VMEM((EDGE, LANE), F32),
        pltpu.VMEM((NODE, D), F32),
        pltpu.VMEM((NODE, D), BF),
        pltpu.VMEM((TABLE, D), F32),
        pltpu.VMEM((NODE, D), F32),
        pltpu.VMEM((D, D), F32),
        pltpu.VMEM((D, D), F32),
        pltpu.VMEM((8, D), F32),
        pltpu.VMEM((NODE, D), F32),
        pltpu.VMEM((2, N_DOM, ROWS, LANE), F32),
        pltpu.SemaphoreType.DMA((NCHUNK,)),
    ]
    return on_device(layer_kernel, outs, scratch, "vvssvvvvvvvvvvvvvv", "avvvvv", 32)(*args)


def finish(rows, own, low, up):
    return on_device(finish_kernel, shape(NODE, D, dtype=BF), [], "vvvv")(rows, own, low, up)


def unpack(core, mine, other):
    outs = (shape(24, D), shape(8, D), shape(16, D), shape(8, D)) + (shape(1, 8),) * 4
    return on_device(unpack_kernel, outs, [], "svv")(core, mine, other)


def swap(values, axis, flip):
    count = lax.axis_size(axis)
    return lax.ppermute(values, axis, [(i, i ^ flip) for i in range(count)])


def per_device(
    node_latent,
    edge_latent,
    node_cot,
    edge_cot,
    edge_w_in,
    edge_b_in,
    edge_w_out,
    edge_gain,
    node_w_in,
    node_b_in,
    node_w_out,
    node_gain,
    edge_senders,
    edge_receivers,
    block_fill,
    send_rows,
):
    node_rows = node_latent[0]
    lists = send_rows[0]
    count = lax.axis_size("dom")
    rise = [(i, i + 1) for i in range(count - 1)]
    fall = [(i + 1, i) for i in range(count - 1)]
    core = lax.rem(lax.axis_index("rep"), 2).reshape(1, 1)
    to_lower, to_upper = pick(lists, node_rows)
    halo_lower = lax.ppermute(to_upper, "dom", rise)
    halo_upper = lax.ppermute(to_lower, "dom", fall)
    half = local(
        edge_senders,
        edge_receivers,
        block_fill,
        edge_latent[0],
        node_rows,
        edge_w_in,
        edge_b_in[None],
    )
    gedge, own, glow, gup, away, kept = layer(
        edge_senders,
        edge_receivers,
        block_fill,
        core,
        half,
        edge_latent[0],
        edge_cot[0],
        node_rows,
        halo_lower,
        halo_upper,
        node_cot[0],
        edge_w_in,
        edge_w_out,
        edge_gain[None],
        node_w_in,
        node_b_in[None],
        node_w_out,
        node_gain[None],
    )
    back_upper = lax.ppermute(glow, "dom", fall)
    back_lower = lax.ppermute(gup, "dom", rise)
    values = (kept + swap(away, "rep", 1).astype(F32)).astype(BF)
    parts = lax.all_to_all(values, "dom", 0, 0, tiled=True)
    values = jnp.sum(parts.astype(F32), 0)
    values, back_lower, back_upper = lax.optimization_barrier((values, back_lower, back_upper))
    others = [swap(values, "rep", flip) for flip in (2, 4, 6)]
    grad_nodes = finish(lists, own, back_lower, back_upper)
    others, grad_nodes = lax.optimization_barrier((others, grad_nodes))
    values = values + others[0] + others[1] + others[2]
    ewi, ewo, nwi, nwo, *vec = unpack(core, values, swap(values, "rep", 1))
    return (
        grad_nodes[None],
        gedge[None],
        ewi,
        vec[0].reshape(8),
        ewo,
        vec[1].reshape(8),
        nwi,
        vec[2].reshape(8),
        nwo,
        vec[3].reshape(8),
    )


def solution(mesh):
    placed = (
        P("rep", "dom", None),
        P("rep", "dom", None),
        P("rep", "dom", None),
        P("rep", "dom", None),
        P(),
        P(),
        P(),
        P(),
        P(),
        P(),
        P(),
        P(),
        P("rep", "dom"),
        P("rep", "dom"),
        P("rep", "dom"),
        P("rep", "dom", None),
    )
    return jax.shard_map(
        per_device,
        mesh=mesh,
        in_specs=placed,
        out_specs=(
            P("rep", "dom", None),
            P("rep", "dom", None),
            P("dom", None),
            P("dom"),
            P("dom", None),
            P("dom"),
            P("dom", None),
            P("dom"),
            P("dom", None),
            P("dom"),
        ),
        check_vma=False,
    )
```

```python
import functools

import jax
import jax.numpy as jnp
from jax import lax
from jax.experimental import pallas as pl
from jax.experimental.pallas import tpu as pltpu
from jax.sharding import PartitionSpec as P

D = 256
NODE = 512
EDGE = 4096
HALO = 128
TABLE = NODE + 2 * HALO
EBLOCK = 128
NBLK = EDGE // EBLOCK
CHUNK = 1024
NCHUNK = EDGE // CHUNK
PER = CHUNK // EBLOCK
LANE = 128
NORM_EPS = 1e-05
N_DOM = 32
ROWS = 64
VECTOR_ROW = 56
WINDOW = 256

BF = jnp.bfloat16
F32 = jnp.float32


def mm(a, b):
    return lax.dot_general(a, b, (((1,), (0,)), ((), ())), preferred_element_type=F32)


def mm_nt(a, b):
    return lax.dot_general(a, b, (((1,), (1,)), ((), ())), preferred_element_type=F32)


def mm_tn(a, b):
    return lax.dot_general(a, b, (((0,), (0,)), ((), ())), preferred_element_type=F32)


def as_columns(row):
    return jnp.broadcast_to(row, (LANE, LANE)).T


def one_hot_rows(row, count):
    places = lax.broadcasted_iota(jnp.int32, (count, row.shape[1]), 0).astype(jnp.int16)
    row = jnp.broadcast_to(row, (16, row.shape[1])).astype(jnp.int16)[0:1]
    return jnp.where(places == row, BF(1.0), BF(0.0))


def one_hot_cols(cols, count):
    places = lax.broadcasted_iota(jnp.int32, (cols.shape[0], LANE), 1).astype(jnp.int16)
    cols = cols.astype(jnp.int16)
    parts = [
        jnp.where(cols == places + jnp.int16(k * LANE), BF(1.0), BF(0.0))
        for k in range(count // LANE)
    ]
    return jnp.concatenate(parts, 1)


def norm_forward(values):
    centred = values - jnp.mean(values, -1, keepdims=True)
    inverse = lax.rsqrt(jnp.mean(centred * centred, -1, keepdims=True) + NORM_EPS)
    return centred * inverse, inverse


def chunk_cols(row, first, count):
    row = row - first
    hots = [
        one_hot_cols(as_columns(row[:, k * LANE : (k + 1) * LANE]), count) for k in range(PER)
    ]
    return jnp.concatenate(hots, 0)


def live_lanes(fill_ref, i):
    lanes = lax.broadcasted_iota(jnp.int32, (1, LANE), 1)
    return jnp.concatenate([lanes < fill_ref[0, i * PER + k] for k in range(PER)], 1)


def chunk_used(fill_ref, i):
    total = fill_ref[0, i * PER]
    for k in range(1, PER):
        total = total + fill_ref[0, i * PER + k]
    return total > 0


def chunk_ids(send_ref, recv_ref, fill_ref, i):
    here = pl.ds(i * CHUNK, CHUNK)
    return send_ref[:, here], jnp.where(live_lanes(fill_ref, i), recv_ref[:, here], -1)


def windows(send_ref, recv_ref, fill_ref):
    firsts, all_fit = [], None
    for i in range(NCHUNK):
        here = pl.ds(i * CHUNK, CHUNK)
        live = live_lanes(fill_ref, i)
        send = send_ref[:, here]
        recv = recv_ref[:, here]
        own = send < NODE
        low = jnp.minimum(recv, jnp.where(own, send, NODE - 1))
        high = jnp.maximum(recv, jnp.where(own, send, 0))
        low = jnp.min(jnp.where(live, low, NODE - 1))
        high = jnp.max(jnp.where(live, high, 0))
        first = jnp.minimum((low // 16) * 16, NODE - WINDOW)
        fits = high < first + WINDOW
        firsts.append(pl.multiple_of(first, 16))
        all_fit = fits if all_fit is None else jnp.logical_and(all_fit, fits)
    return firsts, all_fit


def over_chunks(step, idle, fill_ref, firsts):
    if firsts is not None:
        for i in range(NCHUNK):
            step(i, firsts[i], WINDOW)
        return
    for i in range(NCHUNK - 1):
        step(i, 0, NODE)
    used = chunk_used(fill_ref, NCHUNK - 1)

    @pl.when(used)
    def _():
        step(NCHUNK - 1, 0, NODE)

    @pl.when(jnp.logical_not(used))
    def _():
        idle(NCHUNK - 1)


def either_way(body, send_ref, recv_ref, fill_ref):
    firsts, all_fit = windows(send_ref, recv_ref, fill_ref)

    @pl.when(all_fit)
    def _():
        body(firsts)

    @pl.when(jnp.logical_not(all_fit))
    def _():
        body(None)


def fetch_all(sources, targets, sems):
    copies = [
        pltpu.make_async_copy(source, target, sems.at[k])
        for k, (source, target) in enumerate(zip(sources, targets))
    ]
    for copy in copies:
        copy.start()
    return copies


def pick_kernel(rows_hbm, node_hbm, low_ref, up_ref, rows_ref, node_ref, sems):
    for copy in fetch_all((rows_hbm, node_hbm), (rows_ref, node_ref), sems):
        copy.wait()
    for side, out in ((0, low_ref), (1, up_ref)):
        hot = one_hot_cols(as_columns(rows_ref[side : side + 1, :]), NODE)
        out[...] = mm(hot, node_ref[...]).astype(BF)


def local_kernel(
    send_hbm,
    recv_hbm,
    fill_hbm,
    edge_hbm,
    node_hbm,
    ewi_hbm,
    eb_hbm,
    half_ref,
    send_ref,
    recv_ref,
    fill_ref,
    edge_ref,
    node_ref,
    ewi_ref,
    eb_ref,
    wp_ref,
    sems,
):
    copies = fetch_all(
        (node_hbm, ewi_hbm, eb_hbm, send_hbm, recv_hbm, fill_hbm, edge_hbm),
        (node_ref, ewi_ref, eb_ref, send_ref, recv_ref, fill_ref, edge_ref),
        sems,
    )
    for copy in copies[:-1]:
        copy.wait()
    wp_ref[0:D, :] = (ewi_ref[0:D, :].astype(F32) * 0.5).astype(BF)
    wp_ref[D : D + NODE, :] = (mm(node_ref[...], ewi_ref[D : 2 * D, :]) * 0.5).astype(BF)
    wp_ref[D + NODE :, :] = (
        (mm(node_ref[...], ewi_ref[2 * D :, :]) + eb_ref[...]) * 0.5
    ).astype(BF)

    def step(i, first, width):
        here = pl.ds(i * CHUNK, CHUNK)
        send, recv = chunk_ids(send_ref, recv_ref, fill_ref, i)
        half_ref[here, :] = (
            mm(edge_ref[here, :], wp_ref[0:D, :])
            + mm(chunk_cols(send, first, width), wp_ref[pl.ds(D + first, width), :])
            + mm(chunk_cols(recv, first, width), wp_ref[pl.ds(D + NODE + first, width), :])
        )

    def body(firsts):
        over_chunks(step, lambda i: None, fill_ref, firsts)

    copies[-1].wait()
    either_way(body, send_ref, recv_ref, fill_ref)


def layer_kernel(
    send_ref,
    recv_ref,
    fill_ref,
    core_ref,
    half_ref,
    edge_ref,
    ecot_ref,
    node_ref,
    hlow_ref,
    hup_ref,
    ncot_ref,
    ewi_ref,
    ewo_ref,
    eg_ref,
    nwi_ref,
    nb_ref,
    nwo_ref,
    ng_ref,
    msg_hbm,
    grad_hbm,
    base_ref,
    nsum_ref,
    glow_ref,
    gup_ref,
    away_ref,
    kept_ref,
    msg_ref,
    grad_ref,
    halo_ref,
    hott_ref,
    act_ref,
    normed_ref,
    inv_ref,
    agg_ref,
    back_node_ref,
    sums_ref,
    sumr_ref,
    dw0_ref,
    dwo_ref,
    dgain_ref,
    share_ref,
    sems,
):
    def flush(i):
        here = pl.ds(i * CHUNK, CHUNK)
        return (
            pltpu.make_async_copy(msg_ref.at[here], msg_hbm.at[here], sems.at[0, i]),
            pltpu.make_async_copy(grad_ref.at[here], grad_hbm.at[here], sems.at[1, i]),
        )

    def body(firsts):
        halo = jnp.concatenate([hlow_ref[...], hup_ref[...]], 0)
        halo_ref[...] = (mm(halo, ewi_ref[D : 2 * D, :]) * 0.5).astype(BF)
        agg_ref[...] = jnp.zeros_like(agg_ref)
        gain = eg_ref[...]

        def forward(i, first, width):
            here = pl.ds(i * CHUNK, CHUNK)
            send, recv = chunk_ids(send_ref, recv_ref, fill_ref, i)
            half = half_ref[here, :] + mm(chunk_cols(send, NODE, 2 * HALO), halo_ref[...])
            t = jnp.tanh(half)
            ht = half * t
            act = (half + ht).astype(BF)
            act_ref[here, :] = act
            msg_ref[here, :] = ((t + 1.0) * ((half - ht) + 1.0)).astype(BF)
            normed, inverse = norm_forward(mm(act, ewo_ref[...]))
            normed_ref[here, :] = normed
            inv_ref[here, :] = jnp.broadcast_to(inverse, (CHUNK, LANE))
            message = (edge_ref[here, :].astype(F32) + gain * normed).astype(BF)
            hott = one_hot_rows(recv - first, width)
            if width == WINDOW:
                hott_ref[i] = hott
            agg_ref[pl.ds(first, width), :] += mm(hott, message)

        over_chunks(forward, lambda i: None, fill_ref, firsts)

        both = jnp.concatenate([node_ref[...], agg_ref[...].astype(BF)], 1)
        half = (mm(both, nwi_ref[...]) + nb_ref[...]) * 0.5
        t = jnp.tanh(half)
        ht = half * t
        act = (half + ht).astype(BF)
        slope = (t + 1.0) * ((half - ht) + 1.0) * 0.5
        normed, inverse = norm_forward(mm(act, nwo_ref[...]))
        up = ncot_ref[...].astype(F32)
        c = up * ng_ref[...]
        back = (
            inverse
            * (
                c
                - jnp.mean(c, -1, keepdims=True)
                - normed * jnp.mean(c * normed, -1, keepdims=True)
            )
        ).astype(BF)
        pre_grad = (mm_nt(back, nwo_ref[...]) * slope).astype(BF)
        input_grad = mm_nt(pre_grad, nwi_ref[...])
        base_ref[...] = up + input_grad[:, 0:D]
        back_node_ref[...] = input_grad[:, D:].astype(BF)
        mean = 1.0 / 256.0
        odd = core_ref[0, 0] == 1

        def put(row, block):
            size = block.shape[0] // N_DOM
            block = (block * mean).reshape(N_DOM, size, D)
            left, right = block[:, :, 0:LANE], block[:, :, LANE:]
            kept_ref[:, row : row + size, :] = jnp.where(odd, right, left)
            share_ref[:, row : row + size, :] = jnp.where(odd, left, right)

        put(32, mm_tn(both, pre_grad))
        put(48, mm_tn(act, back))
        node_bias = jnp.sum(pre_grad.astype(F32), 0, keepdims=True)
        node_gain = jnp.sum(up * normed, 0, keepdims=True)

        sums_ref[...] = jnp.zeros_like(sums_ref)
        sumr_ref[...] = jnp.zeros_like(sumr_ref)
        dw0_ref[...] = jnp.zeros_like(dw0_ref)
        dwo_ref[...] = jnp.zeros_like(dwo_ref)
        dgain_ref[...] = jnp.zeros_like(dgain_ref)
        wo_half = (ewo_ref[...].astype(F32) * 0.5).astype(BF)

        def backward(i, first, width):
            here = pl.ds(i * CHUNK, CHUNK)
            send, recv = chunk_ids(send_ref, recv_ref, fill_ref, i)
            slots = lax.broadcasted_iota(jnp.int32, (LANE, D), 0)
            live = jnp.concatenate([slots < fill_ref[0, i * PER + k] for k in range(PER)], 0)
            msg = jnp.where(live, ecot_ref[here, :].astype(F32), 0.0) + mm(
                chunk_cols(recv, first, width), back_node_ref[pl.ds(first, width), :]
            )
            normed = normed_ref[here, :]
            c = msg * gain
            q = c * normed
            dgain_ref[...] += jnp.sum(q.reshape(CHUNK // 8, 8, D), 0)
            inverse = inv_ref[here, :]
            inverse = jnp.concatenate([inverse, inverse], 1)
            back = (
                inverse
                * (c - jnp.mean(c, -1, keepdims=True) - normed * jnp.mean(q, -1, keepdims=True))
            ).astype(BF)
            pre_grad = (mm_nt(back, wo_half) * msg_ref[here, :].astype(F32)).astype(BF)
            msg_ref[here, :] = msg.astype(BF)
            grad_ref[here, :] = pre_grad
            dwo_ref[...] += mm_tn(act_ref[here, :], back)
            dw0_ref[...] += mm_tn(edge_ref[here, :], pre_grad)
            hott = jnp.concatenate(
                [
                    hott_ref[i] if width == WINDOW else one_hot_rows(recv - first, width),
                    one_hot_rows(send - first, width),
                    one_hot_rows(send - NODE, 2 * HALO),
                ],
                0,
            )
            sums = mm(hott, pre_grad)
            sumr_ref[pl.ds(first, width), :] += sums[0:width]
            sums_ref[pl.ds(first, width), :] += sums[width : 2 * width]
            sums_ref[NODE:, :] += sums[2 * width :]
            for copy in flush(i):
                copy.start()

        def padding(i):
            here = pl.ds(i * CHUNK, CHUNK)
            msg_ref[here, :] = jnp.zeros((CHUNK, D), BF)
            grad_ref[here, :] = jnp.zeros((CHUNK, D), BF)
            for copy in flush(i):
                copy.start()

        over_chunks(backward, padding, fill_ref, firsts)

        table = jnp.concatenate([node_ref[...], hlow_ref[...], hup_ref[...]], 0)
        sums = sums_ref[...]
        sumr = sumr_ref[...].astype(BF)
        sums_bf = sums.astype(BF)
        put(
            0,
            jnp.concatenate([dw0_ref[...], mm_tn(table, sums_bf), mm_tn(node_ref[...], sumr)], 0),
        )
        put(24, dwo_ref[...])
        vectors = (
            jnp.sum(sums, 0, keepdims=True),
            jnp.sum(dgain_ref[...], 0, keepdims=True) / gain,
            node_bias,
            node_gain,
        )
        place = lax.broadcasted_iota(jnp.int32, (N_DOM, D), 1) // 8
        mine = place == lax.broadcasted_iota(jnp.int32, (N_DOM, D), 0)
        spread = jnp.concatenate([jnp.where(mine, v * mean, 0.0) for v in vectors], 1)
        source = lax.broadcasted_iota(jnp.int32, (4 * D, LANE), 0)
        target = lax.broadcasted_iota(jnp.int32, (4 * D, LANE), 1)
        moves = jnp.where(target == (source // D) * 8 + source % 8, 1.0, 0.0).astype(BF)
        large = spread.astype(BF)
        row = mm(large, moves) + mm((spread - large.astype(F32)).astype(BF), moves)
        eight = lax.broadcasted_iota(jnp.int32, (N_DOM, 8, LANE), 1)
        rows = jnp.where(eight == 0, row[:, None, :], 0.0)
        kept_ref[:, VECTOR_ROW:, :] = jnp.where(odd, 0.0, rows)
        share_ref[:, VECTOR_ROW:, :] = jnp.where(odd, rows, 0.0)
        away_ref[...] = share_ref[...].astype(BF)
        halo_grad = mm_nt(sums_bf[NODE:], ewi_ref[D : 2 * D, :])
        glow_ref[...] = halo_grad[0:HALO].astype(BF)
        gup_ref[...] = halo_grad[HALO:].astype(BF)
        nsum_ref[:, 0:D] = sums_bf[0:NODE]
        nsum_ref[:, D:] = sumr
        for i in range(NCHUNK):
            for copy in flush(i):
                copy.wait()

    either_way(body, send_ref, recv_ref, fill_ref)


def inputs_kernel(
    msg_hbm,
    grad_hbm,
    base_ref,
    nsum_ref,
    ewi_ref,
    gedge_hbm,
    own_ref,
    msg_ref,
    grad_ref,
    gedge_ref,
    in_sems,
    sems,
):
    def flush(i):
        here = pl.ds(i * CHUNK, CHUNK)
        return pltpu.make_async_copy(gedge_ref.at[here], gedge_hbm.at[here], sems.at[i])

    copies = fetch_all((msg_hbm, grad_hbm), (msg_ref, grad_ref), in_sems)
    own_ref[...] = (
        base_ref[...]
        + mm_nt(nsum_ref[:, 0:D], ewi_ref[D : 2 * D, :])
        + mm_nt(nsum_ref[:, D:], ewi_ref[2 * D :, :])
    )
    for copy in copies:
        copy.wait()
    for i in range(NCHUNK):
        here = pl.ds(i * CHUNK, CHUNK)
        gedge_ref[here, :] = (
            msg_ref[here, :].astype(F32) + mm_nt(grad_ref[here, :], ewi_ref[0:D, :])
        ).astype(BF)
        flush(i).start()
    for i in range(NCHUNK):
        flush(i).wait()


def finish_kernel(rows_ref, own_ref, low_ref, up_ref, out_ref):
    hots = jnp.concatenate(
        [one_hot_rows(rows_ref[0:1, :], NODE), one_hot_rows(rows_ref[1:2, :], NODE)], 1
    )
    parts = jnp.concatenate([low_ref[...], up_ref[...]], 0)
    out_ref[...] = (own_ref[...] + mm(hots, parts)).astype(BF)


def unpack_kernel(core_ref, mine_ref, other_ref, ewi_ref, ewo_ref, nwi_ref, nwo_ref, *vec_refs):
    flip = core_ref[0, 0] == 1
    mine = mine_ref[...]
    other = other_ref[...]
    both = jnp.concatenate([jnp.where(flip, other, mine), jnp.where(flip, mine, other)], 1)
    ewi_ref[...] = both[0:24]
    ewo_ref[...] = both[24:32]
    nwi_ref[...] = both[32:48]
    nwo_ref[...] = both[48:56]
    for k in range(4):
        vec_refs[k][...] = both[VECTOR_ROW : VECTOR_ROW + 1, 8 * k : 8 * k + 8]


def on_device(kernel, outs, scratch, specs, out_specs=None, megabytes=8):
    vmem = pl.BlockSpec(memory_space=pltpu.VMEM)
    kinds = {
        "v": vmem,
        "s": pl.BlockSpec(memory_space=pltpu.SMEM),
        "a": pl.BlockSpec(memory_space=pl.ANY),
        "h": pl.BlockSpec(memory_space=pltpu.HBM),
    }
    flat, tree = jax.tree.flatten(outs)
    out_specs = out_specs or "v" * len(flat)
    return pl.pallas_call(
        kernel,
        out_shape=outs,
        in_specs=[kinds[k] for k in specs],
        out_specs=jax.tree.unflatten(tree, [kinds[k] for k in out_specs]),
        scratch_shapes=scratch,
        compiler_params=pltpu.CompilerParams(vmem_limit_bytes=megabytes * 1024 * 1024),
    )


def in_hbm(*args):
    return [pltpu.with_memory_space_constraint(a, pltpu.HBM) for a in args]


def shape(*dims, dtype=F32):
    return jax.ShapeDtypeStruct(dims, dtype)


def pick(rows, node):
    outs = (shape(HALO, D, dtype=BF),) * 2
    scratch = [
        pltpu.VMEM((2, HALO), jnp.int32),
        pltpu.VMEM((NODE, D), BF),
        pltpu.SemaphoreType.DMA((2,)),
    ]
    return on_device(pick_kernel, outs, scratch, "hh")(*in_hbm(rows, node))


def local(*args):
    scratch = [
        pltpu.VMEM((1, EDGE), jnp.int32),
        pltpu.VMEM((1, EDGE), jnp.int32),
        pltpu.SMEM((1, NBLK), jnp.int32),
        pltpu.VMEM((EDGE, D), BF),
        pltpu.VMEM((NODE, D), BF),
        pltpu.VMEM((3 * D, D), BF),
        pltpu.VMEM((1, D), F32),
        pltpu.VMEM((D + 2 * NODE, D), BF),
        pltpu.SemaphoreType.DMA((7,)),
    ]
    return on_device(local_kernel, shape(EDGE, D), scratch, "hhhhhhh", "v", 10)(*in_hbm(*args))


def layer(*args):
    outs = (
        pltpu.HBM((EDGE, D), BF),
        pltpu.HBM((EDGE, D), BF),
        shape(NODE, D),
        shape(NODE, 2 * D, dtype=BF),
        shape(HALO, D, dtype=BF),
        shape(HALO, D, dtype=BF),
        shape(N_DOM, ROWS, LANE, dtype=BF),
        shape(N_DOM, ROWS, LANE),
    )
    scratch = [
        pltpu.VMEM((EDGE, D), BF),
        pltpu.VMEM((EDGE, D), BF),
        pltpu.VMEM((2 * HALO, D), BF),
        pltpu.VMEM((NCHUNK, WINDOW, CHUNK), BF),
        pltpu.VMEM((EDGE, D), BF),
        pltpu.VMEM((EDGE, D), F32),
        pltpu.VMEM((EDGE, LANE), F32),
        pltpu.VMEM((NODE, D), F32),
        pltpu.VMEM((NODE, D), BF),
        pltpu.VMEM((TABLE, D), F32),
        pltpu.VMEM((NODE, D), F32),
        pltpu.VMEM((D, D), F32),
        pltpu.VMEM((D, D), F32),
        pltpu.VMEM((8, D), F32),
        pltpu.VMEM((N_DOM, ROWS, LANE), F32),
        pltpu.SemaphoreType.DMA((2, NCHUNK)),
    ]
    return on_device(layer_kernel, outs, scratch, "vvssvvvvvvvvvvvvvv", "hhvvvvvv", 30)(*args)


def inputs(*args):
    outs = (shape(EDGE, D, dtype=BF), shape(NODE, D))
    scratch = [pltpu.VMEM((EDGE, D), BF)] * 3 + [
        pltpu.SemaphoreType.DMA((2,)),
        pltpu.SemaphoreType.DMA((NCHUNK,)),
    ]
    return on_device(inputs_kernel, outs, scratch, "hhvvv", "hv", 10)(
        *in_hbm(*args[:2]), *args[2:]
    )


def finish(rows, own, low, up):
    return on_device(finish_kernel, shape(NODE, D, dtype=BF), [], "vvvv")(rows, own, low, up)


def unpack(core, mine, other):
    outs = (shape(24, D), shape(8, D), shape(16, D), shape(8, D)) + (shape(1, 8),) * 4
    return on_device(unpack_kernel, outs, [], "svv")(core, mine, other)


def swap(values, axis, flip):
    count = lax.axis_size(axis)
    return lax.ppermute(values, axis, [(i, i ^ flip) for i in range(count)])


def per_device(
    node_latent,
    edge_latent,
    node_cot,
    edge_cot,
    edge_w_in,
    edge_b_in,
    edge_w_out,
    edge_gain,
    node_w_in,
    node_b_in,
    node_w_out,
    node_gain,
    edge_senders,
    edge_receivers,
    block_fill,
    send_rows,
):
    node_rows = node_latent[0]
    lists = send_rows[0]
    count = lax.axis_size("dom")
    rise = [(i, i + 1) for i in range(count - 1)]
    fall = [(i + 1, i) for i in range(count - 1)]
    core = lax.rem(lax.axis_index("rep"), 2).reshape(1, 1)
    to_lower, to_upper = pick(lists, node_rows)
    halo_lower = lax.ppermute(to_upper, "dom", rise)
    halo_upper = lax.ppermute(to_lower, "dom", fall)
    half = local(
        edge_senders,
        edge_receivers,
        block_fill,
        edge_latent[0],
        node_rows,
        edge_w_in,
        edge_b_in[None],
    )
    msg, grad, base, node_sums, glow, gup, away, kept = layer(
        edge_senders,
        edge_receivers,
        block_fill,
        core,
        half,
        edge_latent[0],
        edge_cot[0],
        node_rows,
        halo_lower,
        halo_upper,
        node_cot[0],
        edge_w_in,
        edge_w_out,
        edge_gain[None],
        node_w_in,
        node_b_in[None],
        node_w_out,
        node_gain[None],
    )
    back_upper = lax.ppermute(glow, "dom", fall)
    back_lower = lax.ppermute(gup, "dom", rise)
    values = (kept + swap(away, "rep", 1).astype(F32)).astype(BF)
    values, msg, grad = lax.optimization_barrier((values, msg, grad))
    parts = lax.all_to_all(values, "dom", 0, 0, tiled=True)
    gedge, own = inputs(msg, grad, base, node_sums, edge_w_in)
    values = jnp.sum(parts.astype(F32), 0)
    values, back_lower, back_upper, own = lax.optimization_barrier(
        (values, back_lower, back_upper, own)
    )
    others = [swap(values, "rep", flip) for flip in (2, 4, 6)]
    grad_nodes = finish(lists, own, back_lower, back_upper)
    others, grad_nodes = lax.optimization_barrier((others, grad_nodes))
    values = values + others[0] + others[1] + others[2]
    ewi, ewo, nwi, nwo, *vec = unpack(core, values, swap(values, "rep", 1))
    return (
        grad_nodes[None],
        gedge[None],
        ewi,
        vec[0].reshape(8),
        ewo,
        vec[1].reshape(8),
        nwi,
        vec[2].reshape(8),
        nwo,
        vec[3].reshape(8),
    )


def solution(mesh):
    placed = (
        P("rep", "dom", None),
        P("rep", "dom", None),
        P("rep", "dom", None),
        P("rep", "dom", None),
        P(),
        P(),
        P(),
        P(),
        P(),
        P(),
        P(),
        P(),
        P("rep", "dom"),
        P("rep", "dom"),
        P("rep", "dom"),
        P("rep", "dom", None),
    )
    return jax.shard_map(
        per_device,
        mesh=mesh,
        in_specs=placed,
        out_specs=(
            P("rep", "dom", None),
            P("rep", "dom", None),
            P("dom", None),
            P("dom"),
            P("dom", None),
            P("dom"),
            P("dom", None),
            P("dom"),
            P("dom", None),
            P("dom"),
        ),
        check_vma=False,
    )
```

```python
import functools

import jax
import jax.numpy as jnp
from jax import lax
from jax.experimental import pallas as pl
from jax.experimental.pallas import tpu as pltpu
from jax.sharding import PartitionSpec as P

D = 256
NODE = 512
EDGE = 4096
HALO = 128
TABLE = NODE + 2 * HALO
EBLOCK = 128
NBLK = EDGE // EBLOCK
CHUNK = 1024
NCHUNK = EDGE // CHUNK
PER = CHUNK // EBLOCK
LANE = 128
NORM_EPS = 1e-05
N_DOM = 32
ROWS = 64
VECTOR_ROW = 56
WINDOW = 256

BF = jnp.bfloat16
F32 = jnp.float32


def mm(a, b):
    return lax.dot_general(a, b, (((1,), (0,)), ((), ())), preferred_element_type=F32)


def mm_nt(a, b):
    return lax.dot_general(a, b, (((1,), (1,)), ((), ())), preferred_element_type=F32)


def mm_tn(a, b):
    return lax.dot_general(a, b, (((0,), (0,)), ((), ())), preferred_element_type=F32)


def as_columns(row):
    return jnp.broadcast_to(row, (LANE, LANE)).T


def one_hot_rows(row, count):
    places = lax.broadcasted_iota(jnp.int32, (count, row.shape[1]), 0).astype(jnp.int16)
    row = jnp.broadcast_to(row, (16, row.shape[1])).astype(jnp.int16)[0:1]
    return jnp.where(places == row, BF(1.0), BF(0.0))


def one_hot_cols(cols, count):
    places = lax.broadcasted_iota(jnp.int32, (cols.shape[0], LANE), 1).astype(jnp.int16)
    cols = cols.astype(jnp.int16)
    parts = [
        jnp.where(cols == places + jnp.int16(k * LANE), BF(1.0), BF(0.0))
        for k in range(count // LANE)
    ]
    return jnp.concatenate(parts, 1)


def norm_forward(values):
    centred = values - jnp.mean(values, -1, keepdims=True)
    inverse = lax.rsqrt(jnp.mean(centred * centred, -1, keepdims=True) + NORM_EPS)
    return centred * inverse, inverse


def chunk_cols(row, first, count):
    row = row - first
    hots = [
        one_hot_cols(as_columns(row[:, k * LANE : (k + 1) * LANE]), count) for k in range(PER)
    ]
    return jnp.concatenate(hots, 0)


def live_lanes(fill_ref, i):
    lanes = lax.broadcasted_iota(jnp.int32, (1, LANE), 1)
    return jnp.concatenate([lanes < fill_ref[0, i * PER + k] for k in range(PER)], 1)


def chunk_used(fill_ref, i):
    total = fill_ref[0, i * PER]
    for k in range(1, PER):
        total = total + fill_ref[0, i * PER + k]
    return total > 0


def chunk_ids(send_ref, recv_ref, fill_ref, i):
    here = pl.ds(i * CHUNK, CHUNK)
    return send_ref[:, here], jnp.where(live_lanes(fill_ref, i), recv_ref[:, here], -1)


def windows(send_ref, recv_ref, fill_ref):
    firsts, all_fit = [], None
    for i in range(NCHUNK):
        here = pl.ds(i * CHUNK, CHUNK)
        live = live_lanes(fill_ref, i)
        send = send_ref[:, here]
        recv = recv_ref[:, here]
        own = send < NODE
        low = jnp.minimum(recv, jnp.where(own, send, NODE - 1))
        high = jnp.maximum(recv, jnp.where(own, send, 0))
        low = jnp.min(jnp.where(live, low, NODE - 1))
        high = jnp.max(jnp.where(live, high, 0))
        first = jnp.minimum((low // 16) * 16, NODE - WINDOW)
        fits = high < first + WINDOW
        firsts.append(pl.multiple_of(first, 16))
        all_fit = fits if all_fit is None else jnp.logical_and(all_fit, fits)
    return firsts, all_fit


def over_chunks(step, idle, fill_ref, firsts):
    if firsts is not None:
        for i in range(NCHUNK):
            step(i, firsts[i], WINDOW)
        return
    for i in range(NCHUNK - 1):
        step(i, 0, NODE)
    used = chunk_used(fill_ref, NCHUNK - 1)

    @pl.when(used)
    def _():
        step(NCHUNK - 1, 0, NODE)

    @pl.when(jnp.logical_not(used))
    def _():
        idle(NCHUNK - 1)


def either_way(body, send_ref, recv_ref, fill_ref):
    firsts, all_fit = windows(send_ref, recv_ref, fill_ref)

    @pl.when(all_fit)
    def _():
        body(firsts)

    @pl.when(jnp.logical_not(all_fit))
    def _():
        body(None)


def fetch_all(sources, targets, sems):
    copies = [
        pltpu.make_async_copy(source, target, sems.at[k])
        for k, (source, target) in enumerate(zip(sources, targets))
    ]
    for copy in copies:
        copy.start()
    return copies


def pick_kernel(rows_hbm, node_hbm, low_ref, up_ref, rows_ref, node_ref, sems):
    for copy in fetch_all((rows_hbm, node_hbm), (rows_ref, node_ref), sems):
        copy.wait()
    for side, out in ((0, low_ref), (1, up_ref)):
        hot = one_hot_cols(as_columns(rows_ref[side : side + 1, :]), NODE)
        out[...] = mm(hot, node_ref[...]).astype(BF)


def local_kernel(
    send_hbm,
    recv_hbm,
    fill_hbm,
    edge_hbm,
    node_hbm,
    ewi_hbm,
    eb_hbm,
    half_ref,
    send_ref,
    recv_ref,
    fill_ref,
    edge_ref,
    node_ref,
    ewi_ref,
    eb_ref,
    wp_ref,
    sems,
):
    copies = fetch_all(
        (node_hbm, ewi_hbm, eb_hbm, send_hbm, recv_hbm, fill_hbm, edge_hbm),
        (node_ref, ewi_ref, eb_ref, send_ref, recv_ref, fill_ref, edge_ref),
        sems,
    )
    for copy in copies[:-1]:
        copy.wait()
    wp_ref[0:D, :] = (ewi_ref[0:D, :].astype(F32) * 0.5).astype(BF)
    wp_ref[D : D + NODE, :] = (mm(node_ref[...], ewi_ref[D : 2 * D, :]) * 0.5).astype(BF)
    wp_ref[D + NODE :, :] = (
        (mm(node_ref[...], ewi_ref[2 * D :, :]) + eb_ref[...]) * 0.5
    ).astype(BF)

    def step(i, first, width):
        here = pl.ds(i * CHUNK, CHUNK)
        send, recv = chunk_ids(send_ref, recv_ref, fill_ref, i)
        half_ref[here, :] = (
            mm(edge_ref[here, :], wp_ref[0:D, :])
            + mm(chunk_cols(send, first, width), wp_ref[pl.ds(D + first, width), :])
            + mm(chunk_cols(recv, first, width), wp_ref[pl.ds(D + NODE + first, width), :])
        )

    def body(firsts):
        over_chunks(step, lambda i: None, fill_ref, firsts)

    copies[-1].wait()
    either_way(body, send_ref, recv_ref, fill_ref)


def layer_kernel(
    send_ref,
    recv_ref,
    fill_ref,
    core_ref,
    half_ref,
    edge_ref,
    ecot_ref,
    node_ref,
    hlow_ref,
    hup_ref,
    ncot_ref,
    ewi_ref,
    ewo_ref,
    eg_ref,
    nwi_ref,
    nb_ref,
    nwo_ref,
    ng_ref,
    msg_hbm,
    grad_hbm,
    base_ref,
    nsum_ref,
    glow_ref,
    gup_ref,
    away_ref,
    kept_ref,
    msg_ref,
    grad_ref,
    halo_ref,
    hott_ref,
    act_ref,
    normed_ref,
    inv_ref,
    agg_ref,
    back_node_ref,
    sums_ref,
    sumr_ref,
    dw0_ref,
    dwo_ref,
    dgain_ref,
    share_ref,
    sems,
):
    def flush(i):
        here = pl.ds(i * CHUNK, CHUNK)
        return (
            pltpu.make_async_copy(msg_ref.at[here], msg_hbm.at[here], sems.at[0, i]),
            pltpu.make_async_copy(grad_ref.at[here], grad_hbm.at[here], sems.at[1, i]),
        )

    def body(firsts):
        halo = jnp.concatenate([hlow_ref[...], hup_ref[...]], 0)
        halo_ref[...] = (mm(halo, ewi_ref[D : 2 * D, :]) * 0.5).astype(BF)
        agg_ref[...] = jnp.zeros_like(agg_ref)
        gain = eg_ref[...]

        def forward(i, first, width):
            here = pl.ds(i * CHUNK, CHUNK)
            send, recv = chunk_ids(send_ref, recv_ref, fill_ref, i)
            half = half_ref[here, :] + mm(chunk_cols(send, NODE, 2 * HALO), halo_ref[...])
            t = jnp.tanh(half)
            ht = half * t
            act = (half + ht).astype(BF)
            act_ref[here, :] = act
            msg_ref[here, :] = ((t + 1.0) * ((half - ht) + 1.0)).astype(BF)
            normed, inverse = norm_forward(mm(act, ewo_ref[...]))
            normed_ref[here, :] = normed
            inv_ref[here, :] = jnp.broadcast_to(inverse, (CHUNK, LANE))
            message = (edge_ref[here, :].astype(F32) + gain * normed).astype(BF)
            hott = one_hot_rows(recv - first, width)
            if width == WINDOW:
                hott_ref[i] = hott
            agg_ref[pl.ds(first, width), :] += mm(hott, message)

        over_chunks(forward, lambda i: None, fill_ref, firsts)

        both = jnp.concatenate([node_ref[...], agg_ref[...].astype(BF)], 1)
        half = (mm(both, nwi_ref[...]) + nb_ref[...]) * 0.5
        t = jnp.tanh(half)
        ht = half * t
        act = (half + ht).astype(BF)
        slope = (t + 1.0) * ((half - ht) + 1.0) * 0.5
        normed, inverse = norm_forward(mm(act, nwo_ref[...]))
        up = ncot_ref[...].astype(F32)
        c = up * ng_ref[...]
        back = (
            inverse
            * (
                c
                - jnp.mean(c, -1, keepdims=True)
                - normed * jnp.mean(c * normed, -1, keepdims=True)
            )
        ).astype(BF)
        pre_grad = (mm_nt(back, nwo_ref[...]) * slope).astype(BF)
        input_grad = mm_nt(pre_grad, nwi_ref[...])
        base_ref[...] = up + input_grad[:, 0:D]
        back_node_ref[...] = input_grad[:, D:].astype(BF)
        mean = 1.0 / 256.0
        odd = core_ref[0, 0] == 1

        def put(row, block):
            size = block.shape[0] // N_DOM
            block = (block * mean).reshape(N_DOM, size, D)
            left, right = block[:, :, 0:LANE], block[:, :, LANE:]
            kept_ref[:, row : row + size, :] = jnp.where(odd, right, left)
            share_ref[:, row : row + size, :] = jnp.where(odd, left, right)

        put(32, mm_tn(both, pre_grad))
        put(48, mm_tn(act, back))
        node_bias = jnp.sum(pre_grad.astype(F32), 0, keepdims=True)
        node_gain = jnp.sum(up * normed, 0, keepdims=True)

        sums_ref[...] = jnp.zeros_like(sums_ref)
        sumr_ref[...] = jnp.zeros_like(sumr_ref)
        dw0_ref[...] = jnp.zeros_like(dw0_ref)
        dwo_ref[...] = jnp.zeros_like(dwo_ref)
        dgain_ref[...] = jnp.zeros_like(dgain_ref)
        wo_half = (ewo_ref[...].astype(F32) * 0.5).astype(BF)

        def backward(i, first, width):
            here = pl.ds(i * CHUNK, CHUNK)
            send, recv = chunk_ids(send_ref, recv_ref, fill_ref, i)
            slots = lax.broadcasted_iota(jnp.int32, (LANE, D), 0)
            live = jnp.concatenate([slots < fill_ref[0, i * PER + k] for k in range(PER)], 0)
            msg = jnp.where(live, ecot_ref[here, :].astype(F32), 0.0) + mm(
                chunk_cols(recv, first, width), back_node_ref[pl.ds(first, width), :]
            )
            normed = normed_ref[here, :]
            c = msg * gain
            q = c * normed
            dgain_ref[...] += jnp.sum(q.reshape(CHUNK // 8, 8, D), 0)
            inverse = inv_ref[here, :]
            inverse = jnp.concatenate([inverse, inverse], 1)
            back = (
                inverse
                * (c - jnp.mean(c, -1, keepdims=True) - normed * jnp.mean(q, -1, keepdims=True))
            ).astype(BF)
            pre_grad = (mm_nt(back, wo_half) * msg_ref[here, :].astype(F32)).astype(BF)
            msg_ref[here, :] = msg.astype(BF)
            grad_ref[here, :] = pre_grad
            dwo_ref[...] += mm_tn(act_ref[here, :], back)
            dw0_ref[...] += mm_tn(edge_ref[here, :], pre_grad)
            hott = jnp.concatenate(
                [
                    hott_ref[i] if width == WINDOW else one_hot_rows(recv - first, width),
                    one_hot_rows(send - first, width),
                    one_hot_rows(send - NODE, 2 * HALO),
                ],
                0,
            )
            sums = mm(hott, pre_grad)
            sumr_ref[pl.ds(first, width), :] += sums[0:width]
            sums_ref[pl.ds(first, width), :] += sums[width : 2 * width]
            sums_ref[NODE:, :] += sums[2 * width :]
            for copy in flush(i):
                copy.start()

        def padding(i):
            here = pl.ds(i * CHUNK, CHUNK)
            msg_ref[here, :] = jnp.zeros((CHUNK, D), BF)
            grad_ref[here, :] = jnp.zeros((CHUNK, D), BF)
            for copy in flush(i):
                copy.start()

        over_chunks(backward, padding, fill_ref, firsts)

        table = jnp.concatenate([node_ref[...], hlow_ref[...], hup_ref[...]], 0)
        sums = sums_ref[...]
        sumr = sumr_ref[...].astype(BF)
        sums_bf = sums.astype(BF)
        put(
            0,
            jnp.concatenate([dw0_ref[...], mm_tn(table, sums_bf), mm_tn(node_ref[...], sumr)], 0),
        )
        put(24, dwo_ref[...])
        vectors = (
            jnp.sum(sums, 0, keepdims=True),
            jnp.sum(dgain_ref[...], 0, keepdims=True) / gain,
            node_bias,
            node_gain,
        )
        place = lax.broadcasted_iota(jnp.int32, (N_DOM, D), 1) // 8
        mine = place == lax.broadcasted_iota(jnp.int32, (N_DOM, D), 0)
        spread = jnp.concatenate([jnp.where(mine, v * mean, 0.0) for v in vectors], 1)
        source = lax.broadcasted_iota(jnp.int32, (4 * D, LANE), 0)
        target = lax.broadcasted_iota(jnp.int32, (4 * D, LANE), 1)
        moves = jnp.where(target == (source // D) * 8 + source % 8, 1.0, 0.0).astype(BF)
        large = spread.astype(BF)
        row = mm(large, moves) + mm((spread - large.astype(F32)).astype(BF), moves)
        eight = lax.broadcasted_iota(jnp.int32, (N_DOM, 8, LANE), 1)
        rows = jnp.where(eight == 0, row[:, None, :], 0.0)
        kept_ref[:, VECTOR_ROW:, :] = jnp.where(odd, 0.0, rows)
        share_ref[:, VECTOR_ROW:, :] = jnp.where(odd, rows, 0.0)
        away_ref[...] = share_ref[...].astype(BF)
        halo_grad = mm_nt(sums_bf[NODE:], ewi_ref[D : 2 * D, :])
        glow_ref[...] = halo_grad[0:HALO].astype(BF)
        gup_ref[...] = halo_grad[HALO:].astype(BF)
        nsum_ref[:, 0:D] = sums_bf[0:NODE]
        nsum_ref[:, D:] = sumr
        for i in range(NCHUNK):
            for copy in flush(i):
                copy.wait()

    either_way(body, send_ref, recv_ref, fill_ref)


def inputs_kernel(
    msg_hbm,
    grad_hbm,
    base_ref,
    nsum_ref,
    ewi_ref,
    gedge_hbm,
    own_ref,
    msg_ref,
    grad_ref,
    gedge_ref,
    in_sems,
    sems,
):
    def flush(i):
        here = pl.ds(i * CHUNK, CHUNK)
        return pltpu.make_async_copy(gedge_ref.at[here], gedge_hbm.at[here], sems.at[i])

    copies = fetch_all((msg_hbm, grad_hbm), (msg_ref, grad_ref), in_sems)
    own_ref[...] = (
        base_ref[...]
        + mm_nt(nsum_ref[:, 0:D], ewi_ref[D : 2 * D, :])
        + mm_nt(nsum_ref[:, D:], ewi_ref[2 * D :, :])
    )
    for copy in copies:
        copy.wait()
    for i in range(NCHUNK):
        here = pl.ds(i * CHUNK, CHUNK)
        gedge_ref[here, :] = (
            msg_ref[here, :].astype(F32) + mm_nt(grad_ref[here, :], ewi_ref[0:D, :])
        ).astype(BF)
        flush(i).start()
    for i in range(NCHUNK):
        flush(i).wait()


def finish_kernel(rows_ref, own_ref, low_ref, up_ref, out_ref):
    hots = jnp.concatenate(
        [one_hot_rows(rows_ref[0:1, :], NODE), one_hot_rows(rows_ref[1:2, :], NODE)], 1
    )
    parts = jnp.concatenate([low_ref[...], up_ref[...]], 0)
    out_ref[...] = (own_ref[...] + mm(hots, parts)).astype(BF)


def unpack_kernel(core_ref, mine_ref, other_ref, ewi_ref, ewo_ref, nwi_ref, nwo_ref, *vec_refs):
    flip = core_ref[0, 0] == 1
    mine = mine_ref[...]
    other = other_ref[...]
    both = jnp.concatenate([jnp.where(flip, other, mine), jnp.where(flip, mine, other)], 1)
    ewi_ref[...] = both[0:24]
    ewo_ref[...] = both[24:32]
    nwi_ref[...] = both[32:48]
    nwo_ref[...] = both[48:56]
    for k in range(4):
        vec_refs[k][...] = both[VECTOR_ROW : VECTOR_ROW + 1, 8 * k : 8 * k + 8]


def on_device(kernel, outs, scratch, specs, out_specs=None, megabytes=8):
    vmem = pl.BlockSpec(memory_space=pltpu.VMEM)
    kinds = {
        "v": vmem,
        "s": pl.BlockSpec(memory_space=pltpu.SMEM),
        "a": pl.BlockSpec(memory_space=pl.ANY),
        "h": pl.BlockSpec(memory_space=pltpu.HBM),
    }
    flat, tree = jax.tree.flatten(outs)
    out_specs = out_specs or "v" * len(flat)
    return pl.pallas_call(
        kernel,
        out_shape=outs,
        in_specs=[kinds[k] for k in specs],
        out_specs=jax.tree.unflatten(tree, [kinds[k] for k in out_specs]),
        scratch_shapes=scratch,
        compiler_params=pltpu.CompilerParams(vmem_limit_bytes=megabytes * 1024 * 1024),
    )


def in_hbm(*args):
    return [pltpu.with_memory_space_constraint(a, pltpu.HBM) for a in args]


def shape(*dims, dtype=F32):
    return jax.ShapeDtypeStruct(dims, dtype)


def pick(rows, node):
    outs = (shape(HALO, D, dtype=BF),) * 2
    scratch = [
        pltpu.VMEM((2, HALO), jnp.int32),
        pltpu.VMEM((NODE, D), BF),
        pltpu.SemaphoreType.DMA((2,)),
    ]
    return on_device(pick_kernel, outs, scratch, "hh")(*in_hbm(rows, node))


def local(*args):
    scratch = [
        pltpu.VMEM((1, EDGE), jnp.int32),
        pltpu.VMEM((1, EDGE), jnp.int32),
        pltpu.SMEM((1, NBLK), jnp.int32),
        pltpu.VMEM((EDGE, D), BF),
        pltpu.VMEM((NODE, D), BF),
        pltpu.VMEM((3 * D, D), BF),
        pltpu.VMEM((1, D), F32),
        pltpu.VMEM((D + 2 * NODE, D), BF),
        pltpu.SemaphoreType.DMA((7,)),
    ]
    return on_device(local_kernel, shape(EDGE, D), scratch, "hhhhhhh", "v", 10)(*in_hbm(*args))


def layer(*args):
    outs = (
        pltpu.HBM((EDGE, D), BF),
        pltpu.HBM((EDGE, D), BF),
        shape(NODE, D),
        shape(NODE, 2 * D, dtype=BF),
        shape(HALO, D, dtype=BF),
        shape(HALO, D, dtype=BF),
        shape(N_DOM, ROWS, LANE, dtype=BF),
        shape(N_DOM, ROWS, LANE),
    )
    scratch = [
        pltpu.VMEM((EDGE, D), BF),
        pltpu.VMEM((EDGE, D), BF),
        pltpu.VMEM((2 * HALO, D), BF),
        pltpu.VMEM((NCHUNK, WINDOW, CHUNK), BF),
        pltpu.VMEM((EDGE, D), BF),
        pltpu.VMEM((EDGE, D), F32),
        pltpu.VMEM((EDGE, LANE), F32),
        pltpu.VMEM((NODE, D), F32),
        pltpu.VMEM((NODE, D), BF),
        pltpu.VMEM((TABLE, D), F32),
        pltpu.VMEM((NODE, D), F32),
        pltpu.VMEM((D, D), F32),
        pltpu.VMEM((D, D), F32),
        pltpu.VMEM((8, D), F32),
        pltpu.VMEM((N_DOM, ROWS, LANE), F32),
        pltpu.SemaphoreType.DMA((2, NCHUNK)),
    ]
    return on_device(layer_kernel, outs, scratch, "vvssvvvvvvvvvvvvvv", "hhvvvvvv", 30)(*args)


def inputs(*args):
    outs = (shape(EDGE, D, dtype=BF), shape(NODE, D))
    scratch = [pltpu.VMEM((EDGE, D), BF)] * 3 + [
        pltpu.SemaphoreType.DMA((2,)),
        pltpu.SemaphoreType.DMA((NCHUNK,)),
    ]
    return on_device(inputs_kernel, outs, scratch, "hhvvv", "hv", 10)(
        *in_hbm(*args[:2]), *args[2:]
    )


def finish(rows, own, low, up):
    return on_device(finish_kernel, shape(NODE, D, dtype=BF), [], "vvvv")(rows, own, low, up)


def unpack(core, mine, other):
    outs = (shape(24, D), shape(8, D), shape(16, D), shape(8, D)) + (shape(1, 8),) * 4
    return on_device(unpack_kernel, outs, [], "svv")(core, mine, other)


def swap(values, axis, flip):
    count = lax.axis_size(axis)
    return lax.ppermute(values, axis, [(i, i ^ flip) for i in range(count)])


def per_device(
    node_latent,
    edge_latent,
    node_cot,
    edge_cot,
    edge_w_in,
    edge_b_in,
    edge_w_out,
    edge_gain,
    node_w_in,
    node_b_in,
    node_w_out,
    node_gain,
    edge_senders,
    edge_receivers,
    block_fill,
    send_rows,
):
    node_rows = node_latent[0]
    lists = send_rows[0]
    count = lax.axis_size("dom")
    rise = [(i, i + 1) for i in range(count - 1)]
    fall = [(i + 1, i) for i in range(count - 1)]
    core = lax.rem(lax.axis_index("rep"), 2).reshape(1, 1)
    to_lower, to_upper = pick(lists, node_rows)
    halo_lower = lax.ppermute(to_upper, "dom", rise)
    halo_upper = lax.ppermute(to_lower, "dom", fall)
    half = local(
        edge_senders,
        edge_receivers,
        block_fill,
        edge_latent[0],
        node_rows,
        edge_w_in,
        edge_b_in[None],
    )
    msg, grad, base, node_sums, glow, gup, away, kept = layer(
        edge_senders,
        edge_receivers,
        block_fill,
        core,
        half,
        edge_latent[0],
        edge_cot[0],
        node_rows,
        halo_lower,
        halo_upper,
        node_cot[0],
        edge_w_in,
        edge_w_out,
        edge_gain[None],
        node_w_in,
        node_b_in[None],
        node_w_out,
        node_gain[None],
    )
    back_upper = lax.ppermute(glow, "dom", fall)
    back_lower = lax.ppermute(gup, "dom", rise)
    values = (kept + swap(away, "rep", 1).astype(F32)).astype(BF)
    values, msg, grad = lax.optimization_barrier((values, msg, grad))
    parts = lax.all_to_all(values, "dom", 0, 0, tiled=True)
    gedge, own = inputs(msg, grad, base, node_sums, edge_w_in)
    values = jnp.sum(parts.astype(F32), 0)
    grad_nodes = finish(lists, own, back_lower, back_upper)
    values, grad_nodes = lax.optimization_barrier((values, grad_nodes))
    others = [swap(values, "rep", flip) for flip in (2, 4, 6)]
    values = values + others[0] + others[1] + others[2]
    ewi, ewo, nwi, nwo, *vec = unpack(core, values, swap(values, "rep", 1))
    return (
        grad_nodes[None],
        gedge[None],
        ewi,
        vec[0].reshape(8),
        ewo,
        vec[1].reshape(8),
        nwi,
        vec[2].reshape(8),
        nwo,
        vec[3].reshape(8),
    )


def solution(mesh):
    placed = (
        P("rep", "dom", None),
        P("rep", "dom", None),
        P("rep", "dom", None),
        P("rep", "dom", None),
        P(),
        P(),
        P(),
        P(),
        P(),
        P(),
        P(),
        P(),
        P("rep", "dom"),
        P("rep", "dom"),
        P("rep", "dom"),
        P("rep", "dom", None),
    )
    return jax.shard_map(
        per_device,
        mesh=mesh,
        in_specs=placed,
        out_specs=(
            P("rep", "dom", None),
            P("rep", "dom", None),
            P("dom", None),
            P("dom"),
            P("dom", None),
            P("dom"),
            P("dom", None),
            P("dom"),
            P("dom", None),
            P("dom"),
        ),
        check_vma=False,
    )
```
